512 devices in a mesh: outer: 16 (over y, z_lo), inner: 8 (over x, core), tensor: 4 (over z_hi).
Axes of the slice: x: 4, y: 4, z: 16 (z_hi: 4, z_lo: 4; z = z_hi * 4 + z_lo), core: 2. Of those that a mesh axis runs over, the one named last changes fastest.
Arguments:
- tokens: bfloat16 [16384, 8192], P(('outer', 'inner', 'tensor')), may hold values from -24 to 24
- ref_codes: bfloat16 [64, 128, 1024], P('inner', None, 'tensor'), may hold values from -4 to 4
- ref_scales: float32 [64, 1024], P('inner', 'tensor'), may hold values from 0.004 to 0.04
- policy_weight: bfloat16 [8192, 1024], P('inner', 'tensor'), may hold values from -0.1875 to 0.1875
- grad_keys: bfloat16 [16384, 1024], P(('outer', 'inner'), 'tensor'), may hold values from -6 to 6
Outputs:
- ref_keys: bfloat16 [16384, 1024], P(('outer', 'inner'), 'tensor')
- grad_weight: float32 [8192, 1024], P(('outer', 'inner'), 'tensor')
- grad_tokens: bfloat16 [16384, 8192], P(('outer', 'inner', 'tensor'))
The draws below stay inside these ranges and needn't reach their ends.
All inputs are finite; a program needn't handle non-finite values.
Results may differ from the reference program's by a relative error of at most 0.013.
Values may be sent and summed in bfloat16 or wider, within the bound.
A program may use at most 64 MiB of HBM per device.

```python
import math
import jax
import jax.numpy as jnp
from jax import lax

D = 8192
QBLOCK = 128
TOK_DEV = 128
KW = 1024
NB = 64
TOKENS = 16384
N_TENSOR = 4


def strengthened(entries, stream_key, source, target, shards_of, factor):
    def block_of(position):
        return (jnp.arange(entries.shape[position]) // (entries.shape[position] // shards_of)).reshape((-1,) + (1,) * (entries.ndim - 1 - position))

    near = jax.random.permutation(stream_key, shards_of)[block_of(target)]
    other_side = (block_of(target) + shards_of // 2) % shards_of
    return jnp.where((block_of(source) == near) | (block_of(source) == other_side), factor * entries, entries)


def steps_of(own_key, shape, split, low, high):
    def one(dim, shards_of):
        steps = jax.random.uniform(jax.random.fold_in(jax.random.fold_in(own_key, 6), dim), (shards_of,), jnp.float32, low / len(split), high / len(split))
        return jnp.repeat(jnp.exp(steps), shape[dim] // shards_of).reshape((-1,) + (1,) * (len(shape) - dim - 1))

    factor_of = one(*split[0])
    for cut in split[1:]:
        factor_of = factor_of * one(*cut)
    return factor_of


def normal_values(stream_key, dims, spread, most, shards=(), held_as=jnp.bfloat16):
    factor_of = steps_of(stream_key, dims, shards, -0.22, 0.18) if shards else 1.0
    values = jax.random.normal(stream_key, dims, jnp.float32) * spread * factor_of
    return jnp.minimum(jnp.maximum(values, -most), most).astype(held_as)


def gaussian_with(key, dims, deviation, most, cuts, heavy, dtype=jnp.bfloat16):
    array = deviation * jax.random.normal(key, dims, jnp.float32)
    if cuts:
        array = array * steps_of(key, dims, cuts, -0.22, 0.18)
    return jnp.clip(strengthened(array, jax.random.fold_in(key, 3), *heavy), -most, most).astype(dtype)


def setup_inputs(seed: int = 0) -> dict:
    key_list = jax.random.split(jax.random.key(seed), 6)
    return {
        "tokens": gaussian_with(key_list[0], (TOKENS, D), 1.0, 24.0, ((0, 512),), (0, 1, 512, 6.0)),
        "ref_codes": normal_values(key_list[1], (NB, QBLOCK, KW), 1.0, 4.0, ((0, 8), (2, 4))),
        "ref_scales": jnp.clip(jnp.exp(math.log(0.04) - 2.30258502 * jax.random.uniform(key_list[2], (NB, KW), jnp.float32) ** steps_of(key_list[2], (NB, KW), ((0, 8), (1, 4)), -0.2, 0.2)), 0.004, 0.04),
        "policy_weight": normal_values(key_list[3], (D, KW), KW ** -0.5, 0.1875, ((0, 8), (1, 4))),
        "grad_keys": normal_values(key_list[4], (TOKENS, KW), 1.0, 6.0, ((0, 128), (1, 4))),
    }


def reference(tokens, ref_codes, ref_scales, policy_weight, grad_keys):
    blocked = jnp.moveaxis(tokens.reshape(TOKENS, NB, QBLOCK), 1, 0)

    def ref_step(carry, inputs):
        columns, codes, scales = inputs
        return (carry + scales[None, :] * jnp.dot(columns, codes, preferred_element_type=jnp.float32), None)
    ref_sum, unused = lax.scan(ref_step, jnp.zeros((TOKENS, KW), jnp.float32), (blocked, ref_codes, ref_scales))
    ref_keys = ref_sum.astype(jnp.bfloat16)
    groups_count = TOKENS // TOK_DEV
    grouped_x = tokens.reshape(groups_count, TOK_DEV, D)
    grouped_g = grad_keys.reshape(groups_count, TOK_DEV, KW)

    def grad_step(carry, inputs):
        group_x, group_g = inputs
        rounded = lax.optimization_barrier(jnp.dot(group_x.T, group_g, preferred_element_type=jnp.float32).astype(jnp.bfloat16))
        return (carry + rounded.astype(jnp.float32), None)
    weight_sum, unused = lax.scan(grad_step, jnp.zeros((D, KW), jnp.float32), (grouped_x, grouped_g))
    grad_weight = weight_sum * lax.rsqrt(jnp.float32(TOKENS))
    width = KW // N_TENSOR
    token_sum = jnp.zeros((TOKENS, D), jnp.float32)
    for block in range(N_TENSOR):
        part = jnp.dot(grad_keys[:, block * width:(block + 1) * width], policy_weight[:, block * width:(block + 1) * width].T, preferred_element_type=jnp.float32)
        rounded = lax.optimization_barrier(part.astype(jnp.bfloat16))
        token_sum = token_sum + rounded.astype(jnp.float32)
    return (ref_keys, grad_weight, token_sum.astype(jnp.bfloat16))
```

```python
import jax
import jax.numpy as jnp
from jax import lax
from jax.experimental import pallas as pl
from jax.experimental.pallas import tpu as pltpu
from jax.sharding import PartitionSpec as P

MESH = pl.DeviceIdType.MESH
F32 = jnp.float32
BF16 = jnp.bfloat16


def remote(src, dst, send_sem, recv_sem, device):
    return pltpu.make_async_remote_copy(
        src_ref=src,
        dst_ref=dst,
        send_sem=send_sem,
        recv_sem=recv_sem,
        device_id=device,
        device_id_type=MESH,
    )


def kernel(
    tok, codes, scales, policy, gkeys,
    keys_out, gw_out, gt_out,
    strips, slab, gk, cw_stage, cw, refs, sib, rs_own, rs, keys_part,
    xt, gwp, gw_send, gw_recv, gw_fin, gt_send, gt_recv,
    tok_s, tok_r, gkz_s, gkz_r, gk_s, gk_r, cwt_s, cwt_r, cw_s, cw_r,
    sib_s, sib_r, rs_s, rs_r, kz_s, kz_r, gw_s, gw_r, gwf_s, gwf_r, gt_s, gt_r,
):
    o = lax.axis_index("outer")
    i = lax.axis_index("inner")
    t = lax.axis_index("tensor")
    y, l = o // 4, o % 4
    x, c = i // 2, i % 2
    chip = y * 4 + x
    me = c * 16 + chip
    z = t * 4 + l

    def plane(p):
        return (((p % 16) // 4) * 4 + l, (p % 4) * 2 + p // 16, t)

    def at_z(zz):
        return (y * 4 + zz % 4, i, zz // 4)

    def at_chip(yy, xx):
        return (yy * 4 + l, xx * 2 + c, t)

    sibling = (o, x * 2 + (1 - c), t)
    up = at_z((z + 1) % 16)
    down = at_z((z + 15) % 16)

    barrier = pltpu.get_barrier_semaphore()

    @pl.loop(1, 32)
    def _(s):
        pl.semaphore_signal(barrier, inc=1, device_id=plane((me + s) % 32), device_id_type=MESH)

    for s in range(1, 4):
        pl.semaphore_signal(barrier, inc=1, device_id=(o, i, (t + s) % 4), device_id_type=MESH)
    pl.semaphore_signal(barrier, inc=1, device_id=up, device_id_type=MESH)
    pl.semaphore_signal(barrier, inc=1, device_id=down, device_id_type=MESH)

    for h in range(2):
        scale = scales[pl.ds(h * 4 + y, 1), :]
        cw_stage[h] = (codes[h * 4 + y].astype(F32) * scale).astype(BF16)
        cw_stage[2 + h] = policy[pl.ds(pl.multiple_of(h * 512 + y * 128, 128), 128), :]
    for p in range(32):
        pc, py, px = p // 16, (p % 16) // 4, p % 4
        for h in range(2):
            col = py * 2048 + (2 * pc + h) * 512 + px * 128
            strips[p, h] = tok[:, col : col + 128]
    slab[me] = strips[me]
    gk[me, t] = gkeys[pl.ds(pl.multiple_of(t * 32, 32), 32), :]

    pl.semaphore_wait(barrier, 36)

    for s in range(1, 4):
        tt = (t + s) % 4
        remote(
            gkeys.at[pl.ds(pl.multiple_of(tt * 32, 32), 32)], gk.at[me, t], gkz_s, gkz_r, (o, i, tt)
        ).start()

    @pl.when(x == y)
    def _():
        for k in range(4):
            cw[t * 4 + k] = cw_stage[k]

    @pl.when(x != y)
    def _():
        for k in range(4):
            remote(cw_stage.at[k], cw.at[t * 4 + k], cwt_s, cwt_r.at[k], at_chip(x, y)).start()

    @pl.loop(1, 32)
    def _(s):
        p = (me + s) % 32
        remote(strips.at[p], slab.at[me], tok_s, tok_r, plane(p)).start()

    remote(gk.at[me, pl.ds(0, 3)], gk.at[me, pl.ds(0, 3)], gkz_s, gkz_r, sibling).wait_recv()

    def a_chip(s):
        return (y + s * c) % 4, (x + s * (1 - c)) % 4

    def b_chip(s):
        return (y + s * (1 - c)) % 4, (x + s * c) % 4

    def gk_send(p, device):
        remote(gk.at[p], gk.at[p], gk_s, gk_r.at[p], device).start()

    def gk_wait(p):
        remote(gk.at[p], gk.at[p], gk_s, gk_r.at[p], sibling).wait_recv()

    for s in range(1, 4):
        gk_send(me, at_chip(*a_chip(s)))
    for s in range(1, 4):
        gk_send(me, at_chip(*b_chip(s)))
    gk_send(me, sibling)

    def cw_to(dirn, m, block, chunk, device):
        k = block * 4 + chunk
        remote(cw.at[k], cw.at[k], cw_s.at[dirn], cw_r.at[dirn, m], device).start()

    for k in range(4):
        @pl.when(x != y)
        def _():
            remote(cw.at[t * 4 + k], cw.at[t * 4 + k], cwt_s, cwt_r.at[k], sibling).wait_recv()

        @pl.when(l == 3)
        def _():
            cw_to(0, k, t, k, up)

        @pl.when(l == 0)
        def _():
            cw_to(1, k, t, k, down)

    def cw_step(m):
        ublock = (t + 3) % 4 if m < 4 else (t + 2) % 4
        uchunk = m if m < 4 else (0, 2)[m - 4]
        dblock = (t + 1) % 4 if m < 4 else (t + 2) % 4
        dchunk = m if m < 4 else (1, 3)[m - 4]
        ku = ublock * 4 + uchunk
        kd = dblock * 4 + dchunk
        remote(cw.at[ku], cw.at[ku], cw_s.at[0], cw_r.at[0, m], up).wait_recv()

        @pl.when(l < 3)
        def _():
            cw_to(0, m, ublock, uchunk, up)

        if m in (0, 2):
            @pl.when(l == 3)
            def _():
                cw_to(0, 4 + m // 2, ublock, uchunk, up)

        remote(cw.at[kd], cw.at[kd], cw_s.at[1], cw_r.at[1, m], down).wait_recv()

        @pl.when(l > 0)
        def _():
            cw_to(1, m, dblock, dchunk, down)

        if m in (1, 3):
            @pl.when(l == 0)
            def _():
                cw_to(1, 4 + m // 2, dblock, dchunk, down)

    def piece(a, b):
        yy = (y + a * c + b * (1 - c)) % 4
        xx = (x + a * (1 - c) + b * c) % 4
        return c * 16 + yy * 4 + xx

    cw_step(0)
    for a in range(1, 4):
        p = piece(a, 0)
        gk_wait(p)
        for s in range(1, 4):
            gk_send(p, at_chip(*b_chip(s)))
        gk_send(p, sibling)
    cw_step(1)
    for a in range(0, 4):
        for b in range(1, 4):
            p = piece(a, b)
            gk_wait(p)
            gk_send(p, sibling)
        if a == 1:
            cw_step(2)
    cw_step(3)

    remote(slab.at[pl.ds(0, 31)], slab.at[pl.ds(0, 31)], tok_s, tok_r, sibling).wait_recv()
    for h in range(2):
        xt[pl.ds(h * 128, 128), :] = slab[:, h].reshape(1024, 128).T

    for k in range(16):
        gk_wait((1 - c) * 16 + k)

    @pl.loop(0, 4)
    def _(tt):
        g = gk[:, tt].reshape(1024, 256)
        part = jnp.dot(xt[...], g, preferred_element_type=F32)
        gwp[tt * 2] = part[:128]
        gwp[tt * 2 + 1] = part[128:]

    def chain(dirn, d):
        zz = (z + d) % 16 if dirn == 0 else (z + 16 - d) % 16
        first = 8 if dirn == 0 else 7
        slot = (zz // 4) * 2 + zz % 2

        @pl.when((zz % 4) // 2 == c)
        def _():
            if d == first:
                gw_send[dirn, slot] = gwp[slot].astype(BF16)
            else:
                remote(
                    gw_recv.at[dirn, slot], gw_recv.at[dirn, slot], gw_s.at[dirn, slot], gw_r.at[dirn, slot], up
                ).wait_recv()
                gw_send[dirn, slot] = (gwp[slot] + gw_recv[dirn, slot].astype(F32)).astype(BF16)
            remote(
                gw_send.at[dirn, slot], gw_recv.at[dirn, slot], gw_s.at[dirn, slot], gw_r.at[dirn, slot],
                up if dirn == 0 else down,
            ).start()

    def chains(d):
        chain(0, d)
        if d < 8:
            chain(1, d)

    chains(8)
    cw_step(4)
    chains(7)
    cw_step(5)

    def code_of(tt):
        return jnp.concatenate([cw[tt * 4], cw[tt * 4 + 1]], axis=0)

    def rows_of(first):
        s = slab[pl.ds(first, 16)]
        return jnp.concatenate([s[:, 0].reshape(512, 128), s[:, 1].reshape(512, 128)], axis=1)

    @pl.loop(0, 4)
    def _(tt):
        part = jnp.dot(rows_of((1 - c) * 16), code_of(tt), preferred_element_type=F32)
        refs[tt] = part.astype(BF16).reshape(16, 32, 256)
        remote(refs.at[tt], sib.at[tt], sib_s, sib_r.at[tt], sibling).start()

    chains(6)

    @pl.loop(0, 4)
    def _(j):
        acc = jnp.zeros((256, 256), F32)
        for tt in range(4):
            g = gk[pl.ds(j * 8, 8), tt].reshape(256, 256)
            w = jnp.concatenate([cw[tt * 4 + 2], cw[tt * 4 + 3]], axis=0)
            acc = acc + lax.dot_general(g, w, (((1,), (1,)), ((), ())), preferred_element_type=F32)
        out = acc.astype(BF16)
        for h in range(2):
            gt_send[pl.ds(j * 8, 8), h] = out[:, h * 128 : (h + 1) * 128].reshape(8, 32, 128)

    gt_recv[me] = gt_send[me]

    @pl.loop(1, 32)
    def _(s):
        p = (me + s) % 32
        remote(gt_send.at[p], gt_recv.at[me], gt_s, gt_r, plane(p)).start()

    chains(5)

    @pl.loop(0, 4)
    def _(tt):
        part = jnp.dot(rows_of(c * 16), code_of(tt), preferred_element_type=F32)
        remote(sib.at[tt], sib.at[tt], sib_s, sib_r.at[tt], sibling).wait_recv()
        total = part.reshape(16, 32, 256) + sib[tt].astype(F32)
        rs_own[:, tt] = total.astype(BF16)

    rs[chip] = rs_own[chip]

    @pl.loop(1, 16)
    def _(s):
        k = (chip + s) % 16
        remote(rs_own.at[k], rs.at[chip], rs_s, rs_r, at_chip(k // 4, k % 4)).start()

    for d in (4, 3, 2, 1):
        chains(d)

    @pl.when(l // 2 == c)
    def _():
        slot = t * 2 + l % 2
        for dirn in range(2):
            remote(
                gw_recv.at[dirn, slot], gw_recv.at[dirn, slot], gw_s.at[dirn, slot], gw_r.at[dirn, slot], up
            ).wait_recv()
        total = gwp[slot] + gw_recv[0, slot].astype(F32) + gw_recv[1, slot].astype(F32)
        total = total * lax.rsqrt(jnp.full((1, 1), 16384.0, F32))
        gw_fin[0] = total[:64]
        gw_fin[1] = total[64:]
        remote(gw_fin.at[1 - c], gw_out, gwf_s, gwf_r, sibling).start()
        gw_out[...] = gw_fin[c]

    remote(rs.at[pl.ds(0, 15)], rs.at[pl.ds(0, 15)], rs_s, rs_r, sibling).wait_recv()
    for tt in range(4):
        acc = rs[0, tt].astype(F32)
        for k in range(1, 16):
            acc = acc + rs[k, tt].astype(F32)
        keys_part[tt] = acc.astype(BF16)
    mine = pl.ds(pl.multiple_of(t * 32, 32), 32)
    keys_out[mine, :] = keys_part[t]
    for s in range(1, 4):
        tt = (t + s) % 4
        remote(keys_part.at[tt], keys_out.at[mine], kz_s, kz_r, (o, i, tt)).start()

    remote(gt_recv.at[pl.ds(0, 31)], gt_recv.at[pl.ds(0, 31)], gt_s, gt_r, sibling).wait_recv()
    for p in range(32):
        pc, py, px = p // 16, (p % 16) // 4, p % 4
        for h in range(2):
            col = py * 2048 + (2 * pc + h) * 512 + px * 128
            gt_out[:, col : col + 128] = gt_recv[p, h]

    @pl.when(l // 2 != c)
    def _():
        remote(gw_fin.at[0], gw_out, gwf_s, gwf_r, sibling).wait_recv()

    @pl.when(l // 2 == c)
    def _():
        remote(gw_fin.at[0], gw_out, gwf_s, gwf_r, sibling).wait_send()

    remote(keys_out.at[pl.ds(0, 96)], keys_out.at[pl.ds(0, 96)], kz_s, kz_r, sibling).wait()
    remote(gkeys.at[pl.ds(0, 96)], gkeys.at[pl.ds(0, 96)], gkz_s, gkz_r, sibling).wait_send()
    remote(strips.at[pl.ds(0, 31)], strips.at[pl.ds(0, 31)], tok_s, tok_r, sibling).wait_send()
    remote(gk.at[pl.ds(0, 31)], gk.at[pl.ds(0, 31)], gk_s, gk_r.at[0], sibling).wait_send()

    @pl.when(x != y)
    def _():
        remote(cw_stage, cw_stage, cwt_s, cwt_r.at[0], sibling).wait_send()

    for dirn in range(2):
        remote(cw.at[pl.ds(0, 6)], cw.at[pl.ds(0, 6)], cw_s.at[dirn], cw_r.at[dirn, 0], sibling).wait_send()
    remote(refs, refs, sib_s, sib_r.at[0], sibling).wait_send()
    remote(rs_own.at[pl.ds(0, 15)], rs_own.at[pl.ds(0, 15)], rs_s, rs_r, sibling).wait_send()
    remote(gt_send.at[pl.ds(0, 31)], gt_send.at[pl.ds(0, 31)], gt_s, gt_r, sibling).wait_send()
    for dirn in range(2):
        for d in range(1, 9 if dirn == 0 else 8):
            zz = (z + d) % 16 if dirn == 0 else (z + 16 - d) % 16
            slot = (zz // 4) * 2 + zz % 2

            @pl.when((zz % 4) // 2 == c)
            def _():
                remote(
                    gw_send.at[dirn, slot], gw_send.at[dirn, slot], gw_s.at[dirn, slot], gw_r.at[dirn, slot], up
                ).wait_send()


def body(tokens, ref_codes, ref_scales, policy_weight, grad_keys):
    vmem = pl.BlockSpec(memory_space=pltpu.VMEM)
    dma = pltpu.SemaphoreType.DMA
    return pl.pallas_call(
        kernel,
        out_shape=(
            jax.ShapeDtypeStruct((128, 256), BF16),
            jax.ShapeDtypeStruct((64, 256), F32),
            jax.ShapeDtypeStruct((32, 8192), BF16),
        ),
        in_specs=[vmem] * 5,
        out_specs=[vmem] * 3,
        scratch_shapes=[
            pltpu.VMEM((32, 2, 32, 128), BF16),
            pltpu.VMEM((32, 2, 32, 128), BF16),
            pltpu.VMEM((32, 4, 32, 256), BF16),
            pltpu.VMEM((4, 128, 256), BF16),
            pltpu.VMEM((16, 128, 256), BF16),
            pltpu.VMEM((4, 16, 32, 256), BF16),
            pltpu.VMEM((4, 16, 32, 256), BF16),
            pltpu.VMEM((16, 4, 32, 256), BF16),
            pltpu.VMEM((16, 4, 32, 256), BF16),
            pltpu.VMEM((4, 32, 256), BF16),
            pltpu.VMEM((256, 1024), BF16),
            pltpu.VMEM((8, 128, 256), F32),
            pltpu.VMEM((2, 8, 128, 256), BF16),
            pltpu.VMEM((2, 8, 128, 256), BF16),
            pltpu.VMEM((2, 64, 256), F32),
            pltpu.VMEM((32, 2, 32, 128), BF16),
            pltpu.VMEM((32, 2, 32, 128), BF16),
            dma, dma, dma, dma,
            dma, dma((32,)),
            dma, dma((4,)),
            dma((2,)), dma((2, 6)),
            dma, dma((4,)),
            dma, dma, dma, dma,
            dma((2, 8)), dma((2, 8)),
            dma, dma, dma, dma,
        ],
        compiler_params=pltpu.CompilerParams(
            collective_id=0, has_side_effects=True, vmem_limit_bytes=48 * 1024 * 1024
        ),
        cost_estimate=pl.CostEstimate(flops=1_700_000_000, bytes_accessed=4_000_000, transcendentals=0),
    )(tokens, ref_codes, ref_scales, policy_weight, grad_keys)


def solution(mesh):
    return jax.shard_map(
        body,
        mesh=mesh,
        in_specs=(
            P(("outer", "inner", "tensor"), None),
            P("inner", None, "tensor"),
            P("inner", "tensor"),
            P("inner", "tensor"),
            P(("outer", "inner"), "tensor"),
        ),
        out_specs=(
            P(("outer", "inner"), "tensor"),
            P(("outer", "inner"), "tensor"),
            P(("outer", "inner", "tensor"), None),
        ),
        check_vma=False,
    )
```

```python
import jax
import jax.numpy as jnp
from jax import lax
from jax.experimental import pallas as pl
from jax.experimental.pallas import tpu as pltpu
from jax.sharding import PartitionSpec as P

MESH = pl.DeviceIdType.MESH
F32 = jnp.float32
BF16 = jnp.bfloat16


def remote(src, dst, send_sem, recv_sem, device):
    return pltpu.make_async_remote_copy(
        src_ref=src,
        dst_ref=dst,
        send_sem=send_sem,
        recv_sem=recv_sem,
        device_id=device,
        device_id_type=MESH,
    )


def among(value, *choices):
    found = value == choices[0]
    for choice in choices[1:]:
        found = found | (value == choice)
    return found


def kernel(
    tok, codes, scales, policy, gkeys,
    keys_out, gw_out, gt_out,
    codes_v, scales_v, gkeys_v, slab, gk, cw, xt, part, rs1, rs1_own, rs2, keys_part,
    gwx, gwx_send, gwx_recv, gwp, gw_send, gw_a, gw_b, gw_fin, gt_send,
    load_s, tok_s, tok_r, gkz_s, gkz_r, gk1_s, gk1_r, gk2_s, gk2_r, cw_s, cw_r, cws_s, cws_r,
    rs1_s, rs1_r, rs2_s, rs2_r, kz_s, kz_r, gwx_s, gwx_r, gw_s, gwa_r, gwb_r, fin_r, gt_s, gt_r,
):
    o = lax.axis_index("outer")
    i = lax.axis_index("inner")
    t = lax.axis_index("tensor")
    y, l = o // 4, o % 4
    x, c = i // 2, i % 2
    z = t * 4 + l
    a = jnp.where(c == 0, x, y)
    b = jnp.where(c == 0, y, x)
    me = a * 4 + b

    def place(aa, bb):
        yy = jnp.where(c == 0, bb, aa)
        xx = jnp.where(c == 0, aa, bb)
        return yy, xx

    def plane(aa, bb):
        yy, xx = place(aa, bb)
        return (yy * 4 + l, xx * 2 + c, t)

    def at_z(zz):
        return (y * 4 + zz % 4, i, zz // 4)

    sibling = (o, x * 2 + (1 - c), t)

    own_l = 2 * c + y // 2

    def final_device(tt, j):
        return (x * 4 + own_l, (2 * (y % 2) + j // 2) * 2 + j % 2, tt)

    def tree_place(tt):
        return (tt * 4 + own_l + 16 - z) % 16

    def is_final(d):
        return among(d, 0, 1, 5, 12, 15)

    def is_self(tt, j):
        fo, fi, ft = final_device(tt, j)
        return (fo == o) & (fi == i) & (ft == t)

    barrier = pltpu.get_barrier_semaphore()

    def greet(device):
        pl.semaphore_signal(barrier, inc=1, device_id=device, device_id_type=MESH)

    @pl.loop(1, 16)
    def _(s):
        k = (me + s) % 16
        greet(plane(k // 4, k % 4))

    greet(sibling)
    for dz in (1, 15, 2, 14, 4, 12, 8, 5, 11):
        greet(at_z((z + dz) % 16))
    src_y = 2 * (l % 2) + x // 2
    src_i = y * 2 + l // 2
    src_self = (src_y == y) & (src_i == i)
    for dz in (11, 15, 1, 4):
        zz = (z + dz) % 16
        greet((src_y * 4 + zz % 4, src_i, zz // 4))

    @pl.when(jnp.logical_not(src_self))
    def _():
        greet((src_y * 4 + l, src_i, t))

    greetings = jnp.int32(25)
    for tt in range(4):
        d = tree_place(tt)
        for j in range(4):
            counts = is_final(d) & jnp.logical_not(is_self(tt, j))
            greetings = greetings + jnp.where(counts, 1, 0)

    slice_cols = x * 2048 + y * 256
    loads = [
        pltpu.make_async_copy(gkeys, gkeys_v, load_s.at[0]),
        pltpu.make_async_copy(codes.at[pl.ds(2 * y, 2)], codes_v, load_s.at[1]),
        pltpu.make_async_copy(scales, scales_v, load_s.at[2]),
    ]
    for h in range(2):
        loads.append(
            pltpu.make_async_copy(
                policy.at[pl.ds(pl.multiple_of(y * 256 + h * 128, 128), 128)],
                cw.at[c * 16 + t * 4 + 2 + h],
                load_s.at[3 + h],
            )
        )
        loads.append(
            pltpu.make_async_copy(
                tok.at[:, pl.ds(pl.multiple_of(slice_cols + h * 1024, 256), 256)],
                slab.at[h, me],
                load_s.at[5 + h],
            )
        )
    for load in loads:
        load.start()
    for load in loads:
        load.wait()
    for h in range(2):
        cw[c * 16 + t * 4 + h] = (codes_v[h].astype(F32) * scales_v[pl.ds(2 * y + h, 1), :]).astype(BF16)
    gk[t, me] = gkeys_v[pl.ds(pl.multiple_of(t * 32, 32), 32), :]

    pl.semaphore_wait(barrier, greetings)

    def cw_copy(dirn, n, k, device):
        return remote(cw.at[k], cw.at[k], cw_s.at[dirn], cw_r.at[dirn, n], device)

    def cw_sibling(k):
        return remote(cw.at[k], cw.at[k], cws_s, cws_r.at[k % 16], sibling)

    own = c * 16 + t * 4
    for n, chunk in ((0, 0), (1, 1), (2, 0), (3, 2), (4, 3), (5, 2)):
        far = n in (2, 5)

        @pl.when(l == 3)
        def _():
            cw_copy(0, n, own + chunk, at_z((z + (5 if far else 1)) % 16)).start()

        @pl.when(l == 0)
        def _():
            cw_copy(1, n, own + chunk + (1 if far else 0), at_z((z + (11 if far else 15)) % 16)).start()

    for s in (2, 1, 3):
        tt = (t + s) % 4
        remote(
            gkeys_v.at[pl.ds(pl.multiple_of(tt * 32, 32), 32)], gk.at[t, me], gkz_s, gkz_r.at[s], (o, i, tt)
        ).start()

    def gk_first(tt):
        for s in range(1, 4):
            remote(gk.at[tt, me], gk.at[tt, me], gk1_s, gk1_r.at[tt, s], plane(a, (b + s) % 4)).start()

    def gk_second(tt):
        for s in range(1, 4):
            k = a * 4 + (b + 4 - s) % 4
            remote(gk.at[tt, k], gk.at[tt, k], gk1_s, gk1_r.at[tt, s], sibling).wait_recv()
        rows = gk.at[tt, pl.ds(a * 4, 4)]
        for s in range(1, 4):
            remote(rows, rows, gk2_s, gk2_r.at[tt, s], plane((a + s) % 4, b)).start()

    def gk_done(tt):
        for s in range(1, 4):
            rows = gk.at[tt, pl.ds((a + 4 - s) % 4 * 4, 4)]
            remote(rows, rows, gk2_s, gk2_r.at[tt, s], sibling).wait_recv()

    def gk_exchanged(s):
        tt = (t + 4 - s) % 4
        remote(gk.at[tt, me], gk.at[tt, me], gkz_s, gkz_r.at[s], sibling).wait_recv()
        gk_first(tt)

    gk_first(t)

    @pl.loop(1, 16)
    def _(s):
        k = (me + s) % 16
        yy, xx = place(k // 4, k % 4)
        for h in range(2):
            cols = pl.ds(pl.multiple_of(xx * 2048 + yy * 256 + h * 1024, 256), 256)
            remote(tok.at[:, cols], slab.at[h, me], tok_s, tok_r.at[h], plane(k // 4, k % 4)).start()

    for chunk in range(4):
        cw_sibling(own + chunk).start()

    def cw_step(dirn, n):
        far = n % 3 == 2
        third = n // 3
        chunk = jnp.where(far, 2 * third + dirn, n - third)
        step = jnp.where(far, 2, 1)
        block = (t + 4 - step) % 4 if dirn == 0 else (t + step) % 4
        k = c * 16 + block * 4 + chunk
        cw_copy(dirn, n, k, sibling).wait_recv()

        @pl.when((l < 3) if dirn == 0 else (l > 0))
        def _():
            cw_copy(dirn, n, k, at_z((z + (1 if dirn == 0 else 15)) % 16)).start()

        cw_sibling(k).start()

    def tick(s):
        n_up = s - 2 * l
        n_down = s - 2 * (3 - l)

        @pl.when((n_up >= 0) & (n_up < 6))
        def _():
            cw_step(0, n_up)

        @pl.when((n_down >= 0) & (n_down < 6))
        def _():
            cw_step(1, n_down)

    def codes_of(h, tt):
        k = h * 16 + tt * 4
        return jnp.concatenate([cw[k], cw[k + 1]], axis=0)

    def policy_of(h, tt):
        k = h * 16 + tt * 4 + 2
        return jnp.concatenate([cw[k], cw[k + 1]], axis=0)

    def sibling_chunks(tt, first):
        for chunk in (first, first + 1):
            k = (1 - c) * 16 + tt * 4 + chunk
            cw_sibling(k).wait_recv()

    def gw_part(tt):
        gk_done(tt)
        out = jnp.dot(xt[...], gk[tt].reshape(512, 256), preferred_element_type=F32)
        gwx[0] = out[:256]
        gwx[1] = out[256:]
        gwx_send[tt] = gwx[1 - c].astype(BF16)
        remote(gwx_send.at[tt], gwx_recv.at[tt], gwx_s, gwx_r.at[tt], sibling).start()
        gwp[tt] = gwx[c]

    def gw_first(tt):
        remote(gwx_send.at[tt], gwx_recv.at[tt], gwx_s, gwx_r.at[tt], sibling).wait_recv()
        gwp[tt] = gwp[tt] + gwx_recv[tt].astype(F32)
        d = tree_place(tt)
        down = among(d, 9, 11, 13)

        @pl.when(among(d, 2, 4, 6, 8) | down)
        def _():
            gw_send[tt] = gwp[tt].astype(BF16)
            remote(
                gw_send.at[tt], gw_a.at[tt], gw_s.at[tt, 4], gwa_r.at[tt], at_z((z + jnp.where(down, 15, 1)) % 16)
            ).start()

    def gw_add_a(tt):
        remote(gw_send.at[tt], gw_a.at[tt], gw_s.at[tt, 4], gwa_r.at[tt], sibling).wait_recv()
        gwp[tt] = gwp[tt] + gw_a[tt].astype(F32)

    def gw_second(tt):
        d = tree_place(tt)

        @pl.when(among(d, 3, 7, 10, 14))
        def _():
            gw_add_a(tt)
            gw_send[tt] = gwp[tt].astype(BF16)
            dz = jnp.where(d == 10, 14, jnp.where(d == 14, 15, 2))
            remote(gw_send.at[tt], gw_b.at[tt], gw_s.at[tt, 4], gwb_r.at[tt], at_z((z + dz) % 16)).start()

    def gw_third(tt):
        d = tree_place(tt)

        @pl.when(is_final(d))
        def _():
            @pl.when(among(d, 1, 5, 12))
            def _():
                gw_add_a(tt)

            @pl.when(among(d, 1, 5, 12, 15))
            def _():
                remote(gw_send.at[tt], gw_b.at[tt], gw_s.at[tt, 4], gwb_r.at[tt], sibling).wait_recv()
                gwp[tt] = gwp[tt] + gw_b[tt].astype(F32)

            gw_send[tt] = gwp[tt].astype(BF16)
            slot = jnp.where(d == 1, 1, jnp.where(d == 5, 2, jnp.where(d == 12, 3, jnp.where(d == 15, 4, 0))))
            for j in range(4):
                rows = gw_send.at[tt, pl.ds(j * 64, 64)]

                @pl.when(is_self(tt, j))
                def _():
                    gw_fin[0] = gw_send[tt, j * 64 : (j + 1) * 64]

                @pl.when(jnp.logical_not(is_self(tt, j)))
                def _():
                    remote(rows, gw_fin.at[slot], gw_s.at[tt, j], fin_r.at[slot], final_device(tt, j)).start()

    def ref_part(tt):
        out = jnp.dot(slab[0].reshape(512, 256), codes_of(0, tt), preferred_element_type=F32)
        out = out + jnp.dot(slab[1].reshape(512, 256), codes_of(1, tt), preferred_element_type=F32)
        part[tt] = out.astype(BF16).reshape(16, 32, 256)
        for s in range(1, 4):
            aa = (a + s) % 4
            remote(part.at[tt, pl.ds(aa * 4, 4)], rs1.at[tt, s - 1], rs1_s, rs1_r.at[tt, s], plane(aa, b)).start()

    def ref_second(tt):
        total = part[tt, pl.ds(a * 4, 4)].astype(F32)
        for s in range(1, 4):
            remote(rs1.at[tt, s - 1], rs1.at[tt, s - 1], rs1_s, rs1_r.at[tt, s], sibling).wait_recv()
            total = total + rs1[tt, s - 1].astype(F32)
        rs1_own[tt] = total.astype(BF16)
        for s in range(1, 4):
            bb = (b + s) % 4
            remote(rs1_own.at[tt, bb], rs2.at[tt, s - 1], rs2_s, rs2_r.at[tt, s], plane(a, bb)).start()

    mine = pl.ds(pl.multiple_of(t * 32, 32), 32)

    def ref_third(s):
        tt = (t + s) % 4
        total = rs1_own[tt, b].astype(F32)
        for q in range(1, 4):
            remote(rs2.at[tt, q - 1], rs2.at[tt, q - 1], rs2_s, rs2_r.at[tt, q], sibling).wait_recv()
            total = total + rs2[tt, q - 1].astype(F32)
        keys_part[tt] = total.astype(BF16)
        if s == 0:
            keys_out[mine, :] = keys_part[t]
        else:
            remote(keys_part.at[tt], keys_out.at[mine], kz_s, kz_r, (o, i, tt)).start()

    tick(0)
    gk_second(t)
    tick(1)
    gk_exchanged(1)
    gk_exchanged(3)
    tick(2)
    tick(3)
    gk_exchanged(2)
    gk_second((t + 3) % 4)
    gk_second((t + 1) % 4)
    tick(4)
    for h in range(2):
        remote(
            slab.at[h, pl.ds(0, 15)], slab.at[h, pl.ds(0, 15)], tok_s, tok_r.at[h], sibling
        ).wait_recv()
    for h in range(2):
        xt[pl.ds(h * 256, 256), :] = slab[h].reshape(512, 256).T
    gw_part(t)
    gk_second((t + 2) % 4)
    tick(5)
    sibling_chunks(t, 0)
    ref_part(t)
    tick(6)
    gw_part((t + 3) % 4)
    gw_part((t + 1) % 4)
    tick(7)
    for s in (3, 1):
        tt = (t + s) % 4
        sibling_chunks(tt, 0)
        ref_part(tt)
    tick(8)
    gw_part((t + 2) % 4)
    for s in (0, 3, 1):
        gw_first((t + s) % 4)
    tick(9)
    sibling_chunks((t + 2) % 4, 0)
    ref_part((t + 2) % 4)
    gw_first((t + 2) % 4)
    tick(10)
    ref_second(t)
    tick(11)
    for s in (3, 1):
        ref_second((t + s) % 4)

    for tt in range(4):
        sibling_chunks(tt, 2)

    @pl.loop(0, 2)
    def _(j):
        rows = [gk[tt, pl.ds(j * 8, 8)].reshape(256, 256) for tt in range(4)]
        for h in range(2):
            acc = jnp.zeros((256, 256), F32)
            for tt in range(4):
                acc = acc + lax.dot_general(
                    rows[tt], policy_of(h, tt), (((1,), (1,)), ((), ())), preferred_element_type=F32
                )
            gt_send[h, pl.ds(j * 8, 8)] = acc.astype(BF16).reshape(8, 32, 256)

    def gt_cols(h):
        return pl.ds(pl.multiple_of(slice_cols + h * 1024, 256), 256)

    @pl.loop(1, 16)
    def _(s):
        k = (me + s) % 16
        for h in range(2):
            remote(gt_send.at[h, k], gt_out.at[:, gt_cols(h)], gt_s, gt_r, plane(k // 4, k % 4)).start()

    gt_own = [pltpu.make_async_copy(gt_send.at[h, me], gt_out.at[:, gt_cols(h)], load_s.at[h]) for h in range(2)]
    for copy in gt_own:
        copy.start()

    for tt in range(4):
        gw_second(tt)
    ref_second((t + 2) % 4)
    for s in (0, 3, 1):
        ref_third(s)
    for tt in range(4):
        gw_third(tt)
    ref_third(2)

    total = jnp.zeros((64, 256), F32)
    for slot in range(5):
        def arrived():
            remote(gw_fin.at[slot], gw_fin.at[slot], gw_s.at[0, 0], fin_r.at[slot], sibling).wait_recv()

        if slot == 0:
            pl.when(jnp.logical_not(src_self))(arrived)
        else:
            arrived()
        total = total + gw_fin[slot].astype(F32)
    gw_out[...] = total * lax.rsqrt(jnp.full((1, 1), 16384.0, F32))

    for copy in gt_own:
        copy.wait()
    gt_all = gt_out.at[:, pl.ds(0, 30 * 256)]
    remote(gt_all, gt_all, gt_s, gt_r, sibling).wait_recv()
    remote(keys_out.at[pl.ds(0, 96)], keys_out.at[pl.ds(0, 96)], kz_s, kz_r, sibling).wait()
    remote(gkeys_v.at[pl.ds(0, 96)], gkeys_v.at[pl.ds(0, 96)], gkz_s, gkz_r.at[0], sibling).wait_send()
    remote(gt_all, gt_all, tok_s, tok_r.at[0], sibling).wait_send()
    remote(gt_all, gt_all, gt_s, gt_r, sibling).wait_send()
    remote(gk.at[0, pl.ds(0, 12)], gk.at[0, pl.ds(0, 12)], gk1_s, gk1_r.at[0, 0], sibling).wait_send()
    remote(gk.at[pl.ds(0, 3)], gk.at[pl.ds(0, 3)], gk2_s, gk2_r.at[0, 0], sibling).wait_send()
    remote(part.at[pl.ds(0, 3)], part.at[pl.ds(0, 3)], rs1_s, rs1_r.at[0, 0], sibling).wait_send()
    remote(rs2, rs2, rs2_s, rs2_r.at[0, 0], sibling).wait_send()
    for dirn in range(2):
        remote(cw.at[pl.ds(0, 6)], cw.at[pl.ds(0, 6)], cw_s.at[dirn], cw_r.at[dirn, 0], sibling).wait_send()
    remote(cw.at[pl.ds(0, 16)], cw.at[pl.ds(0, 16)], cws_s, cws_r.at[0], sibling).wait_send()
    remote(gwx_send, gwx_send, gwx_s, gwx_r.at[0], sibling).wait_send()
    for tt in range(4):
        final = is_final(tree_place(tt))

        @pl.when(jnp.logical_not(final))
        def _():
            remote(gw_send.at[tt], gw_send.at[tt], gw_s.at[tt, 4], gwa_r.at[tt], sibling).wait_send()

        for j in range(4):
            rows = gw_send.at[tt, pl.ds(j * 64, 64)]

            @pl.when(final & jnp.logical_not(is_self(tt, j)))
            def _():
                remote(rows, rows, gw_s.at[tt, j], gwa_r.at[tt], sibling).wait_send()


def body(tokens, ref_codes, ref_scales, policy_weight, grad_keys):
    vmem = pl.BlockSpec(memory_space=pltpu.VMEM)
    hbm = pl.BlockSpec(memory_space=pltpu.HBM)
    dma = pltpu.SemaphoreType.DMA
    return pl.pallas_call(
        kernel,
        out_shape=(
            jax.ShapeDtypeStruct((128, 256), BF16),
            jax.ShapeDtypeStruct((64, 256), F32),
            jax.ShapeDtypeStruct((32, 8192), BF16),
        ),
        in_specs=[hbm] * 5,
        out_specs=[vmem, vmem, hbm],
        scratch_shapes=[
            pltpu.VMEM((2, 128, 256), BF16),
            pltpu.VMEM((8, 256), F32),
            pltpu.VMEM((128, 256), BF16),
            pltpu.VMEM((2, 16, 32, 256), BF16),
            pltpu.VMEM((4, 16, 32, 256), BF16),
            pltpu.VMEM((32, 128, 256), BF16),
            pltpu.VMEM((512, 512), BF16),
            pltpu.VMEM((4, 16, 32, 256), BF16),
            pltpu.VMEM((4, 3, 4, 32, 256), BF16),
            pltpu.VMEM((4, 4, 32, 256), BF16),
            pltpu.VMEM((4, 3, 32, 256), BF16),
            pltpu.VMEM((4, 32, 256), BF16),
            pltpu.VMEM((2, 256, 256), F32),
            pltpu.VMEM((4, 256, 256), BF16),
            pltpu.VMEM((4, 256, 256), BF16),
            pltpu.VMEM((4, 256, 256), F32),
            pltpu.VMEM((4, 256, 256), BF16),
            pltpu.VMEM((4, 256, 256), BF16),
            pltpu.VMEM((4, 256, 256), BF16),
            pltpu.VMEM((5, 64, 256), BF16),
            pltpu.VMEM((2, 16, 32, 256), BF16),
            dma((7,)),
            dma, dma((2,)),
            dma, dma((4,)),
            dma, dma((4, 4)), dma, dma((4, 4)),
            dma((2,)), dma((2, 6)), dma, dma((16,)),
            dma, dma((4, 4)), dma, dma((4, 4)),
            dma, dma,
            dma, dma((4,)),
            dma((4, 5)), dma((4,)), dma((4,)), dma((5,)),
            dma, dma,
        ],
        compiler_params=pltpu.CompilerParams(
            collective_id=0, has_side_effects=True, vmem_limit_bytes=48 * 1024 * 1024
        ),
        cost_estimate=pl.CostEstimate(flops=1_700_000_000, bytes_accessed=4_000_000, transcendentals=0),
    )(tokens, ref_codes, ref_scales, policy_weight, grad_keys)


def solution(mesh):
    return jax.shard_map(
        body,
        mesh=mesh,
        in_specs=(
            P(("outer", "inner", "tensor"), None),
            P("inner", None, "tensor"),
            P("inner", "tensor"),
            P("inner", "tensor"),
            P(("outer", "inner"), "tensor"),
        ),
        out_specs=(
            P(("outer", "inner"), "tensor"),
            P(("outer", "inner"), "tensor"),
            P(("outer", "inner", "tensor"), None),
        ),
        check_vma=False,
    )
```

```python
import jax
import jax.numpy as jnp
from jax import lax
from jax.experimental import pallas as pl
from jax.experimental.pallas import tpu as pltpu
from jax.sharding import PartitionSpec as P

MESH = pl.DeviceIdType.MESH
F32 = jnp.float32
BF16 = jnp.bfloat16


CHUNKS = ((0, 1, 2, 3), (1, 0, 3, 2))
STARTS = (0, 2, 4, 7, 8, 13)


def remote(src, dst, send_sem, recv_sem, device):
    return pltpu.make_async_remote_copy(
        src_ref=src,
        dst_ref=dst,
        send_sem=send_sem,
        recv_sem=recv_sem,
        device_id=device,
        device_id_type=MESH,
    )


def among(value, *choices):
    found = value == choices[0]
    for choice in choices[1:]:
        found = found | (value == choice)
    return found


def kernel(
    tok, codes, scales, policy, gkeys,
    keys_out, gw_out, gt_out,
    codes_v, scales_v, gkeys_v, slab, gk, cw, xt, part, rs1, rs1_own, rs2, keys_part,
    gwx_send, gwx_recv, gwp, gw_send, gw_a, gw_b, gw_fin, gt_send,
    load_s, tok_s, tok_r, gkz_s, gkz_r, gk1_s, gk1_r, gk2_s, gk2_r, gkd_s, gkd_r, cw_s, cw_r, cws_s, cws_r,
    rs1_s, rs1_r, rs2_s, rs2_r, kz_s, kz_r, gwx_s, gwx_r, gw_s, gwa_r, gwb_r, fin_r, gt_s, gt_r,
    near_in, far_in,
):
    o = lax.axis_index("outer")
    i = lax.axis_index("inner")
    t = lax.axis_index("tensor")
    y, l = o // 4, o % 4
    x, c = i // 2, i % 2
    z = t * 4 + l
    a = jnp.where(c == 0, x, y)
    b = jnp.where(c == 0, y, x)
    me = a * 4 + b

    def place(aa, bb):
        yy = jnp.where(c == 0, bb, aa)
        xx = jnp.where(c == 0, aa, bb)
        return yy, xx

    def plane(aa, bb):
        yy, xx = place(aa, bb)
        return (yy * 4 + l, xx * 2 + c, t)

    def at_z(zz):
        return (y * 4 + zz % 4, i, zz // 4)

    sibling = (o, x * 2 + (1 - c), t)

    own_l = 2 * c + y // 2

    def final_device(tt, j):
        return (x * 4 + own_l, (2 * (y % 2) + j // 2) * 2 + j % 2, tt)

    def tree_place(tt, q):
        d = (tt * 4 + own_l + 16 - z) % 16
        return d if q == 0 else (16 - d) % 16

    def tree_device(dz, q):
        return at_z((z + (dz if q == 0 else 16 - dz)) % 16)

    def is_final(d):
        return among(d, 0, 1, 5, 12, 15)

    def is_self(tt, j):
        fo, fi, ft = final_device(tt, j)
        return (fo == o) & (fi == i) & (ft == t)

    barrier = pltpu.get_barrier_semaphore()

    def greet(device):
        pl.semaphore_signal(barrier, inc=1, device_id=device, device_id_type=MESH)

    @pl.loop(1, 16)
    def _(s):
        k = (me + s) % 16
        greet(plane(k // 4, k % 4))

    greet(sibling)
    for dz in (1, 15, 4, 12):
        greet(at_z((z + dz) % 16))

    slice_cols = x * 2048 + y * 256
    loads = [
        pltpu.make_async_copy(gkeys, gkeys_v, load_s.at[0]),
        pltpu.make_async_copy(codes.at[pl.ds(2 * y, 2)], codes_v, load_s.at[1]),
        pltpu.make_async_copy(scales, scales_v, load_s.at[2]),
    ]
    for h in range(2):
        loads.append(
            pltpu.make_async_copy(
                policy.at[pl.ds(pl.multiple_of(y * 256 + h * 128, 128), 128)],
                cw.at[c * 16 + t * 4 + 2 + h],
                load_s.at[3 + h],
            )
        )
        loads.append(
            pltpu.make_async_copy(
                tok.at[:, pl.ds(pl.multiple_of(slice_cols + h * 1024, 256), 256)],
                slab.at[h, me],
                load_s.at[5 + h],
            )
        )
    for load in loads:
        load.start()
    for load in loads:
        load.wait()
    for h in range(2):
        cw[c * 16 + t * 4 + h] = (codes_v[h].astype(F32) * scales_v[pl.ds(2 * y + h, 1), :]).astype(BF16)
    gk[t, me] = gkeys_v[pl.ds(pl.multiple_of(t * 32, 32), 32), :]

    pl.semaphore_wait(barrier, 20)

    def tell(sem, device):
        pl.semaphore_signal(sem, inc=1, device_id=device, device_id_type=MESH)

    tell(near_in, sibling)
    for dz in (1, 15, 4, 12):
        tell(near_in, at_z((z + dz) % 16))

    def heard_near():
        pl.semaphore_wait(near_in, 5)
        for dz in (1, 15, 4, 12, 5, 11):
            tell(far_in, at_z((z + dz) % 16))

    def heard_far():
        pl.semaphore_wait(far_in, 6)

    def cw_copy(dirn, n, k, device):
        return remote(cw.at[k], cw.at[k], cw_s.at[dirn], cw_r.at[dirn, n], device)

    def cw_sibling(k):
        return remote(cw.at[k], cw.at[k], cws_s, cws_r.at[k % 16], sibling)

    def gk_send(s):
        tt = (t + s) % 4
        remote(
            gkeys_v.at[pl.ds(pl.multiple_of(tt * 32, 32), 32)], gk.at[t, me], gkz_s, gkz_r.at[s], (o, i, tt)
        ).start()

    gk_send(1)
    gk_send(3)

    def gk_first(tt):
        for s in range(1, 4):
            remote(gk.at[tt, me], gk.at[tt, me], gk1_s, gk1_r.at[tt, s], plane(a, (b + s) % 4)).start()

    def gk_second(tt):
        for s in range(1, 4):
            k = a * 4 + (b + 4 - s) % 4
            remote(gk.at[tt, k], gk.at[tt, k], gk1_s, gk1_r.at[tt, s], sibling).wait_recv()
        rows = gk.at[tt, pl.ds(a * 4, 4)]
        for s in range(1, 4):
            remote(rows, rows, gk2_s, gk2_r.at[tt, s], plane((a + s) % 4, b)).start()

    def gk_done(tt, direct=False):
        if direct:
            rows = gk.at[tt, pl.ds(0, 15)]
            remote(rows, rows, gkd_s, gkd_r, sibling).wait_recv()
            return
        for s in range(1, 4):
            rows = gk.at[tt, pl.ds((a + 4 - s) % 4 * 4, 4)]
            remote(rows, rows, gk2_s, gk2_r.at[tt, s], sibling).wait_recv()

    def gk_direct(tt):
        @pl.loop(1, 16)
        def _(s):
            k = (me + s) % 16
            remote(gk.at[tt, me], gk.at[tt, me], gkd_s, gkd_r, plane(k // 4, k % 4)).start()

    def gk_exchanged(s):
        tt = (t + 4 - s) % 4
        remote(gk.at[tt, me], gk.at[tt, me], gkz_s, gkz_r.at[s], sibling).wait_recv()
        if s == 2:
            gk_direct(tt)
        else:
            gk_first(tt)

    gk_first(t)

    own = c * 16 + t * 4
    for n in range(4):
        @pl.when(l == 3)
        def _():
            cw_copy(0, n, own + CHUNKS[0][n], at_z((z + 1) % 16)).start()

        @pl.when(l == 0)
        def _():
            cw_copy(1, n, own + CHUNKS[1][n], at_z((z + 15) % 16)).start()

    @pl.loop(1, 16)
    def _(s):
        k = (me + s) % 16
        yy, xx = place(k // 4, k % 4)
        for h in range(2):
            cols = pl.ds(pl.multiple_of(xx * 2048 + yy * 256 + h * 1024, 256), 256)
            remote(tok.at[:, cols], slab.at[h, me], tok_s, tok_r.at[h], plane(k // 4, k % 4)).start()

    for chunk in range(4):
        cw_sibling(own + chunk).start()

    def cw_step(dirn, n, steps):
        far = n >= 4
        block = (t + (2 if far else 3 if dirn == 0 else 1)) % 4
        k = c * 16 + block * 4 + CHUNKS[dirn][2 * (n - 4) if far else n]
        onward = 1 if dirn == 0 else 15
        cw_copy(dirn, n, k, sibling).wait_recv()
        if steps < 3:
            cw_copy(dirn, n, k, at_z((z + onward) % 16)).start()
        if steps == 0 and n in (0, 2):
            cw_copy(dirn, 4 + n // 2, k, at_z((z + 4 * onward) % 16)).start()
        cw_sibling(k).start()

    def tick(s):
        for chip in range(4):
            for dirn, steps in ((0, chip), (1, 3 - chip)):
                for n, start in enumerate(STARTS):
                    if start + 5 * steps == s:
                        @pl.when(l == chip)
                        def _():
                            cw_step(dirn, n, steps)

    def codes_of(h, tt):
        k = h * 16 + tt * 4
        return jnp.concatenate([cw[k], cw[k + 1]], axis=0)

    def policy_of(h, tt):
        k = h * 16 + tt * 4 + 2
        return jnp.concatenate([cw[k], cw[k + 1]], axis=0)

    def sibling_chunks(tt, first):
        for chunk in (first, first + 1):
            k = (1 - c) * 16 + tt * 4 + chunk
            cw_sibling(k).wait_recv()

    def gw_part(s):
        tt = (t + s) % 4
        gk_done(tt, s == 2)
        g = gk[tt].reshape(512, 256)
        gwx_send[tt] = jnp.dot(xt[1 - c], g, preferred_element_type=F32).astype(BF16).reshape(2, 128, 256)
        remote(gwx_send.at[tt], gwx_recv.at[tt], gwx_s, gwx_r.at[tt], sibling).start()
        gwp[tt] = jnp.dot(xt[c], g, preferred_element_type=F32).reshape(2, 128, 256)

    def gw_first(tt):
        remote(gwx_send.at[tt], gwx_recv.at[tt], gwx_s, gwx_r.at[tt], sibling).wait_recv()
        for q in range(2):
            gwp[tt, q] = gwp[tt, q] + gwx_recv[tt, q].astype(F32)
            d = tree_place(tt, q)
            down = among(d, 9, 11, 13)

            @pl.when(among(d, 2, 4, 6, 8) | down)
            def _():
                gw_send[tt, q] = gwp[tt, q].astype(BF16)
                remote(
                    gw_send.at[tt, q], gw_a.at[tt, q], gw_s.at[tt, q, 2], gwa_r.at[tt, q],
                    tree_device(jnp.where(down, 15, 1), q),
                ).start()

    def gw_add_a(tt, q):
        remote(gw_send.at[tt, q], gw_a.at[tt, q], gw_s.at[tt, q, 2], gwa_r.at[tt, q], sibling).wait_recv()
        gwp[tt, q] = gwp[tt, q] + gw_a[tt, q].astype(F32)

    def gw_second(tt):
        for q in range(2):
            d = tree_place(tt, q)

            @pl.when(among(d, 3, 7, 10, 14))
            def _():
                gw_add_a(tt, q)
                gw_send[tt, q] = gwp[tt, q].astype(BF16)
                dz = jnp.where(d == 10, 14, jnp.where(d == 14, 15, 2))
                remote(
                    gw_send.at[tt, q], gw_b.at[tt, q], gw_s.at[tt, q, 2], gwb_r.at[tt, q], tree_device(dz, q)
                ).start()

    def gw_third(tt):
        for q in range(2):
            d = tree_place(tt, q)

            @pl.when(is_final(d))
            def _():
                @pl.when(among(d, 1, 5, 12))
                def _():
                    gw_add_a(tt, q)

                @pl.when(among(d, 1, 5, 12, 15))
                def _():
                    remote(
                        gw_send.at[tt, q], gw_b.at[tt, q], gw_s.at[tt, q, 2], gwb_r.at[tt, q], sibling
                    ).wait_recv()
                    gwp[tt, q] = gwp[tt, q] + gw_b[tt, q].astype(F32)

                gw_send[tt, q] = gwp[tt, q].astype(BF16)
                slot = jnp.where(d == 1, 1, jnp.where(d == 5, 2, jnp.where(d == 12, 3, jnp.where(d == 15, 4, 0))))
                for e in range(2):
                    j = 2 * q + e

                    @pl.when(is_self(tt, j))
                    def _():
                        gw_fin[0] = gw_send[tt, q, e * 64 : (e + 1) * 64]

                    @pl.when(jnp.logical_not(is_self(tt, j)))
                    def _():
                        remote(
                            gw_send.at[tt, q, pl.ds(e * 64, 64)], gw_fin.at[slot], gw_s.at[tt, q, e],
                            fin_r.at[slot], final_device(tt, j),
                        ).start()

    def ref_part(tt):
        rows = jnp.concatenate([slab[0].reshape(512, 256), slab[1].reshape(512, 256)], axis=1)
        both = jnp.concatenate([codes_of(0, tt), codes_of(1, tt)], axis=0)
        out = jnp.dot(rows, both, preferred_element_type=F32)
        part[tt] = out.astype(BF16).reshape(16, 32, 256)
        for s in range(1, 4):
            aa = (a + s) % 4
            remote(part.at[tt, pl.ds(aa * 4, 4)], rs1.at[tt, s - 1], rs1_s, rs1_r.at[tt, s], plane(aa, b)).start()

    def ref_second(tt):
        total = part[tt, pl.ds(a * 4, 4)].astype(F32)
        for s in range(1, 4):
            remote(rs1.at[tt, s - 1], rs1.at[tt, s - 1], rs1_s, rs1_r.at[tt, s], sibling).wait_recv()
            total = total + rs1[tt, s - 1].astype(F32)
        rs1_own[tt] = total.astype(BF16)
        for s in range(1, 4):
            bb = (b + s) % 4
            remote(rs1_own.at[tt, bb], rs2.at[tt, s - 1], rs2_s, rs2_r.at[tt, s], plane(a, bb)).start()

    mine = pl.ds(pl.multiple_of(t * 32, 32), 32)

    def ref_third(s):
        tt = (t + s) % 4
        total = rs1_own[tt, b].astype(F32)
        for q in range(1, 4):
            remote(rs2.at[tt, q - 1], rs2.at[tt, q - 1], rs2_s, rs2_r.at[tt, q], sibling).wait_recv()
            total = total + rs2[tt, q - 1].astype(F32)
        keys_part[tt] = total.astype(BF16)
        if isinstance(s, int) and s == 0:
            keys_out[mine, :] = keys_part[t]
        else:
            remote(keys_part.at[tt], keys_out.at[mine], kz_s, kz_r, (o, i, tt)).start()

    def tokens_done():
        for h in range(2):
            remote(
                slab.at[h, pl.ds(0, 15)], slab.at[h, pl.ds(0, 15)], tok_s, tok_r.at[h], sibling
            ).wait_recv()
        for h in range(2):
            xt[h] = slab[h].reshape(512, 256).T

    first = jnp.where(l < 2, 3, 1)
    second = 4 - first

    def ref(s):
        tt = (t + s) % 4
        sibling_chunks(tt, 0)
        ref_part(tt)

    def gt_cols(h):
        return pl.ds(pl.multiple_of(slice_cols + h * 1024, 256), 256)

    gt_own = [pltpu.make_async_copy(gt_send.at[h, me], gt_out.at[:, gt_cols(h)], load_s.at[h]) for h in range(2)]

    def grad_tokens():
        for tt in range(4):
            sibling_chunks(tt, 2)

        @pl.loop(0, 2)
        def _(j):
            rows = [gk[tt, pl.ds(j * 8, 8)].reshape(256, 256) for tt in range(4)]
            for h in range(2):
                acc = jnp.zeros((256, 256), F32)
                for tt in range(4):
                    acc = acc + lax.dot_general(
                        rows[tt], policy_of(h, tt), (((1,), (1,)), ((), ())), preferred_element_type=F32
                    )
                gt_send[h, pl.ds(j * 8, 8)] = acc.astype(BF16).reshape(8, 32, 256)

    def gt_sends():
        @pl.loop(1, 16)
        def _(s):
            k = (me + s) % 16
            for h in range(2):
                remote(gt_send.at[h, k], gt_out.at[:, gt_cols(h)], gt_s, gt_r, plane(k // 4, k % 4)).start()

        for copy in gt_own:
            copy.start()

    gk_second(t)
    tick(0)
    heard_near()
    gk_send(2)
    gk_exchanged(1)
    gk_exchanged(3)
    tick(2)
    tick(4)
    tick(5)
    gk_second((t + 3) % 4)
    gk_second((t + 1) % 4)
    gk_exchanged(2)
    tick(7)
    tokens_done()
    tick(8)
    tick(9)
    gw_part(0)
    tick(10)
    ref(0)
    tick(12)
    tick(13)
    gw_part(3)
    gw_first(t)
    tick(14)
    gw_part(1)
    tick(15)
    gw_part(2)
    gw_first((t + 3) % 4)
    tick(17)
    gw_first((t + 1) % 4)
    ref(first)
    gw_first((t + 2) % 4)
    ref_second(t)
    tick(18)
    tick(19)
    ref(second)
    ref_second((t + first) % 4)
    gw_second(t)
    gw_second((t + 2) % 4)
    gw_second((t + 3) % 4)
    gw_second((t + 1) % 4)
    tick(22)
    tick(23)
    ref(2)
    ref_second((t + second) % 4)
    heard_far()
    tick(28)
    gw_third(t)
    gw_third((t + 3) % 4)
    gw_third((t + 1) % 4)
    gw_third((t + 2) % 4)
    grad_tokens()
    ref_second((t + 2) % 4)
    ref_third(0)
    ref_third(first)
    gt_sends()
    ref_third(second)
    ref_third(2)

    src_self = (2 * (l % 2) + x // 2 == y) & (y * 2 + l // 2 == i)
    total = jnp.zeros((64, 256), F32)
    for slot in range(5):
        def arrived():
            remote(gw_fin.at[slot], gw_fin.at[slot], gw_s.at[0, 0, 0], fin_r.at[slot], sibling).wait_recv()

        if slot == 0:
            pl.when(jnp.logical_not(src_self))(arrived)
        else:
            arrived()
        total = total + gw_fin[slot].astype(F32)
    gw_out[...] = total * lax.rsqrt(jnp.full((1, 1), 16384.0, F32))

    for copy in gt_own:
        copy.wait()
    gt_all = gt_out.at[:, pl.ds(0, 30 * 256)]
    remote(gt_all, gt_all, gt_s, gt_r, sibling).wait_recv()
    remote(keys_out.at[pl.ds(0, 96)], keys_out.at[pl.ds(0, 96)], kz_s, kz_r, sibling).wait()
    remote(gkeys_v.at[pl.ds(0, 96)], gkeys_v.at[pl.ds(0, 96)], gkz_s, gkz_r.at[0], sibling).wait_send()
    remote(gt_all, gt_all, tok_s, tok_r.at[0], sibling).wait_send()
    remote(gt_all, gt_all, gt_s, gt_r, sibling).wait_send()
    remote(gk.at[0, pl.ds(0, 9)], gk.at[0, pl.ds(0, 9)], gk1_s, gk1_r.at[0, 0], sibling).wait_send()
    remote(gk.at[0, pl.ds(0, 15)], gk.at[0, pl.ds(0, 15)], gkd_s, gkd_r, sibling).wait_send()
    remote(rs1.at[pl.ds(0, 3)], rs1.at[pl.ds(0, 3)], gk2_s, gk2_r.at[0, 0], sibling).wait_send()
    remote(part.at[pl.ds(0, 3)], part.at[pl.ds(0, 3)], rs1_s, rs1_r.at[0, 0], sibling).wait_send()
    remote(rs2, rs2, rs2_s, rs2_r.at[0, 0], sibling).wait_send()
    for dirn, steps in ((0, l), (1, 3 - l)):
        for sent, here in ((4, steps == 3), (8, steps == 0), (6, among(steps, 1, 2))):
            @pl.when(here)
            def _():
                rows = cw.at[pl.ds(0, sent)]
                remote(rows, rows, cw_s.at[dirn], cw_r.at[dirn, 0], sibling).wait_send()
    remote(cw.at[pl.ds(0, 16)], cw.at[pl.ds(0, 16)], cws_s, cws_r.at[0], sibling).wait_send()
    remote(gwx_send, gwx_send, gwx_s, gwx_r.at[0], sibling).wait_send()
    for tt in range(4):
        for q in range(2):
            final = is_final(tree_place(tt, q))

            @pl.when(jnp.logical_not(final))
            def _():
                remote(gw_send.at[tt, q], gw_send.at[tt, q], gw_s.at[tt, q, 2], gwa_r.at[tt, q], sibling).wait_send()

            for e in range(2):
                rows = gw_send.at[tt, q, pl.ds(e * 64, 64)]

                @pl.when(final & jnp.logical_not(is_self(tt, 2 * q + e)))
                def _():
                    remote(rows, rows, gw_s.at[tt, q, e], gwa_r.at[tt, q], sibling).wait_send()


def body(tokens, ref_codes, ref_scales, policy_weight, grad_keys):
    vmem = pl.BlockSpec(memory_space=pltpu.VMEM)
    hbm = pl.BlockSpec(memory_space=pltpu.HBM)
    dma = pltpu.SemaphoreType.DMA
    return pl.pallas_call(
        kernel,
        out_shape=(
            jax.ShapeDtypeStruct((128, 256), BF16),
            jax.ShapeDtypeStruct((64, 256), F32),
            jax.ShapeDtypeStruct((32, 8192), BF16),
        ),
        in_specs=[hbm] * 5,
        out_specs=[vmem, vmem, hbm],
        scratch_shapes=[
            pltpu.VMEM((2, 128, 256), BF16),
            pltpu.VMEM((8, 256), F32),
            pltpu.VMEM((128, 256), BF16),
            pltpu.VMEM((2, 16, 32, 256), BF16),
            pltpu.VMEM((4, 16, 32, 256), BF16),
            pltpu.VMEM((32, 128, 256), BF16),
            pltpu.VMEM((2, 256, 512), BF16),
            pltpu.VMEM((4, 16, 32, 256), BF16),
            pltpu.VMEM((4, 3, 4, 32, 256), BF16),
            pltpu.VMEM((4, 4, 32, 256), BF16),
            pltpu.VMEM((4, 3, 32, 256), BF16),
            pltpu.VMEM((4, 32, 256), BF16),
            pltpu.VMEM((4, 2, 128, 256), BF16),
            pltpu.VMEM((4, 2, 128, 256), BF16),
            pltpu.VMEM((4, 2, 128, 256), F32),
            pltpu.VMEM((4, 2, 128, 256), BF16),
            pltpu.VMEM((4, 2, 128, 256), BF16),
            pltpu.VMEM((4, 2, 128, 256), BF16),
            pltpu.VMEM((5, 64, 256), BF16),
            pltpu.VMEM((2, 16, 32, 256), BF16),
            dma((7,)),
            dma, dma((2,)),
            dma, dma((4,)),
            dma, dma((4, 4)), dma, dma((4, 4)), dma, dma,
            dma((2,)), dma((2, 6)), dma, dma((16,)),
            dma, dma((4, 4)), dma, dma((4, 4)),
            dma, dma,
            dma, dma((4,)),
            dma((4, 2, 3)), dma((4, 2)), dma((4, 2)), dma((5,)),
            dma, dma,
            pltpu.SemaphoreType.REGULAR, pltpu.SemaphoreType.REGULAR,
        ],
        compiler_params=pltpu.CompilerParams(
            collective_id=0, has_side_effects=True, vmem_limit_bytes=64 * 1024 * 1024 - 256 * 1024
        ),
        cost_estimate=pl.CostEstimate(flops=1_700_000_000, bytes_accessed=4_000_000, transcendentals=0),
    )(tokens, ref_codes, ref_scales, policy_weight, grad_keys)


def solution(mesh):
    return jax.shard_map(
        body,
        mesh=mesh,
        in_specs=(
            P(("outer", "inner", "tensor"), None),
            P("inner", None, "tensor"),
            P("inner", "tensor"),
            P("inner", "tensor"),
            P(("outer", "inner"), "tensor"),
        ),
        out_specs=(
            P(("outer", "inner"), "tensor"),
            P(("outer", "inner"), "tensor"),
            P(("outer", "inner", "tensor"), None),
        ),
        check_vma=False,
    )
```

```python
import jax
import jax.numpy as jnp
from jax import lax
from jax.experimental import pallas as pl
from jax.experimental.pallas import tpu as pltpu
from jax.sharding import PartitionSpec as P

MESH = pl.DeviceIdType.MESH
F32 = jnp.float32
BF16 = jnp.bfloat16


CHUNKS = ((0, 1, 2, 3), (1, 0, 3, 2))
STARTS = (0, 2, 4, 7, 8, 13)


def remote(src, dst, send_sem, recv_sem, device):
    return pltpu.make_async_remote_copy(
        src_ref=src,
        dst_ref=dst,
        send_sem=send_sem,
        recv_sem=recv_sem,
        device_id=device,
        device_id_type=MESH,
    )


def among(value, *choices):
    found = value == choices[0]
    for choice in choices[1:]:
        found = found | (value == choice)
    return found


def kernel(
    tok, codes, scales, policy, gkeys,
    keys_out, gw_out, gt_out,
    codes_v, scales_v, gkeys_v, slab, gk, cw, xt, part, rs1, rs1_own, rs2, keys_part,
    gwx_send, gwx_recv, gwp, gw_send, gw_a, gw_b, gw_fin, gt_send,
    load_s, tok_s, tok_r, gkz_s, gkz_r, gk1_s, gk1_r, gk2_s, gk2_r, gkd_s, gkd_r, cw_s, cw_r, cws_s, cws_r,
    rs1_s, rs1_r, rs2_s, rs2_r, kz_s, kz_r, gwx_s, gwx_r, gw_s, gwa_r, gwb_r, fin_r, gt_s, gt_r,
    near_in, far_in, gk_relay, relay_s, relay_r, passed_r,
):
    o = lax.axis_index("outer")
    i = lax.axis_index("inner")
    t = lax.axis_index("tensor")
    y, l = o // 4, o % 4
    x, c = i // 2, i % 2
    z = t * 4 + l
    a = jnp.where(c == 0, x, y)
    b = jnp.where(c == 0, y, x)
    me = a * 4 + b

    def place(aa, bb):
        yy = jnp.where(c == 0, bb, aa)
        xx = jnp.where(c == 0, aa, bb)
        return yy, xx

    def plane(aa, bb):
        yy, xx = place(aa, bb)
        return (yy * 4 + l, xx * 2 + c, t)

    def at_z(zz):
        return (y * 4 + zz % 4, i, zz // 4)

    sibling = (o, x * 2 + (1 - c), t)

    own_l = 2 * c + y // 2

    def final_device(tt, j):
        return (x * 4 + own_l, (2 * (y % 2) + j // 2) * 2 + j % 2, tt)

    def tree_place(tt, q):
        d = (tt * 4 + own_l + 16 - z) % 16
        return d if q == 0 else (16 - d) % 16

    def tree_device(dz, q):
        return at_z((z + (dz if q == 0 else 16 - dz)) % 16)

    def is_final(d):
        return among(d, 0, 1, 5, 12, 15)

    def is_self(tt, j):
        fo, fi, ft = final_device(tt, j)
        return (fo == o) & (fi == i) & (ft == t)

    barrier = pltpu.get_barrier_semaphore()

    def greet(device):
        pl.semaphore_signal(barrier, inc=1, device_id=device, device_id_type=MESH)

    @pl.loop(1, 16)
    def _(s):
        k = (me + s) % 16
        greet(plane(k // 4, k % 4))

    greet(sibling)
    for dz in (1, 15, 4, 12):
        greet(at_z((z + dz) % 16))

    slice_cols = x * 2048 + y * 256
    loads = [
        pltpu.make_async_copy(gkeys, gkeys_v, load_s.at[0]),
        pltpu.make_async_copy(codes.at[pl.ds(2 * y, 2)], codes_v, load_s.at[1]),
        pltpu.make_async_copy(scales, scales_v, load_s.at[2]),
    ]
    for h in range(2):
        loads.append(
            pltpu.make_async_copy(
                policy.at[pl.ds(pl.multiple_of(y * 256 + h * 128, 128), 128)],
                cw.at[c * 16 + t * 4 + 2 + h],
                load_s.at[3 + h],
            )
        )
        loads.append(
            pltpu.make_async_copy(
                tok.at[:, pl.ds(pl.multiple_of(slice_cols + h * 1024, 256), 256)],
                slab.at[h, me],
                load_s.at[5 + h],
            )
        )
    for load in loads:
        load.start()
    for load in loads:
        load.wait()
    for h in range(2):
        cw[c * 16 + t * 4 + h] = (codes_v[h].astype(F32) * scales_v[pl.ds(2 * y + h, 1), :]).astype(BF16)
    gk[t, me] = gkeys_v[pl.ds(pl.multiple_of(t * 32, 32), 32), :]

    pl.semaphore_wait(barrier, 20)

    def tell(sem, device):
        pl.semaphore_signal(sem, inc=1, device_id=device, device_id_type=MESH)

    tell(near_in, sibling)
    for dz in (1, 15, 4, 12):
        tell(near_in, at_z((z + dz) % 16))

    def heard_near():
        pl.semaphore_wait(near_in, 5)
        for dz in (1, 15, 4, 12, 5, 11):
            tell(far_in, at_z((z + dz) % 16))

    def heard_far():
        pl.semaphore_wait(far_in, 6)

    def cw_copy(dirn, n, k, device):
        return remote(cw.at[k], cw.at[k], cw_s.at[dirn], cw_r.at[dirn, n], device)

    def cw_sibling(k):
        return remote(cw.at[k], cw.at[k], cws_s, cws_r.at[k % 16], sibling)

    def gk_send(s):
        tt = (t + s) % 4
        remote(
            gkeys_v.at[pl.ds(pl.multiple_of(tt * 32, 32), 32)], gk.at[t, me], gkz_s, gkz_r.at[s], (o, i, tt)
        ).start()

    gk_send(1)
    gk_send(3)

    def relay_rows(n):
        return pl.ds(pl.multiple_of((t + 2) % 4 * 32 + n * 16, 16), 16)

    for n, s in ((0, 1), (1, 3)):
        remote(gkeys_v.at[relay_rows(n)], gk_relay.at[n], gkz_s, relay_r.at[n], (o, i, (t + s) % 4)).start()

    def gk_landing(tt, n):
        return gk.at[tt, me, pl.ds(n * 16, 16)]

    def gk_passed_on():
        for n, s in ((0, 1), (1, 3)):
            remote(gk_relay.at[n], gk_relay.at[n], gkz_s, relay_r.at[n], sibling).wait_recv()
            remote(
                gk_relay.at[n], gk_landing((t + 4 - s) % 4, n), relay_s, passed_r.at[n], (o, i, (t + s) % 4)
            ).start()

    def gk_first(tt):
        for s in range(1, 4):
            remote(gk.at[tt, me], gk.at[tt, me], gk1_s, gk1_r.at[tt, s], plane(a, (b + s) % 4)).start()

    def gk_second(tt):
        for s in range(1, 4):
            k = a * 4 + (b + 4 - s) % 4
            remote(gk.at[tt, k], gk.at[tt, k], gk1_s, gk1_r.at[tt, s], sibling).wait_recv()
        rows = gk.at[tt, pl.ds(a * 4, 4)]
        for s in range(1, 4):
            remote(rows, rows, gk2_s, gk2_r.at[tt, s], plane((a + s) % 4, b)).start()

    def gk_done(tt, direct=False):
        if direct:
            rows = gk.at[tt, pl.ds(0, 15)]
            remote(rows, rows, gkd_s, gkd_r, sibling).wait_recv()
            return
        for s in range(1, 4):
            rows = gk.at[tt, pl.ds((a + 4 - s) % 4 * 4, 4)]
            remote(rows, rows, gk2_s, gk2_r.at[tt, s], sibling).wait_recv()

    def gk_direct(tt):
        @pl.loop(1, 16)
        def _(s):
            k = (me + s) % 16
            remote(gk.at[tt, me], gk.at[tt, me], gkd_s, gkd_r, plane(k // 4, k % 4)).start()

    def gk_exchanged(s):
        tt = (t + 4 - s) % 4
        if s == 2:
            for n in range(2):
                remote(gk_landing(tt, n), gk_landing(tt, n), gkz_s, passed_r.at[n], sibling).wait_recv()
            gk_direct(tt)
        else:
            remote(gk.at[tt, me], gk.at[tt, me], gkz_s, gkz_r.at[s], sibling).wait_recv()
            gk_first(tt)

    gk_first(t)

    own = c * 16 + t * 4
    for n in range(4):
        @pl.when(l == 3)
        def _():
            cw_copy(0, n, own + CHUNKS[0][n], at_z((z + 1) % 16)).start()

        @pl.when(l == 0)
        def _():
            cw_copy(1, n, own + CHUNKS[1][n], at_z((z + 15) % 16)).start()

    @pl.loop(1, 16)
    def _(s):
        k = (me + s) % 16
        yy, xx = place(k // 4, k % 4)
        for h in range(2):
            cols = pl.ds(pl.multiple_of(xx * 2048 + yy * 256 + h * 1024, 256), 256)
            remote(tok.at[:, cols], slab.at[h, me], tok_s, tok_r.at[h], plane(k // 4, k % 4)).start()

    for chunk in range(4):
        cw_sibling(own + chunk).start()

    def cw_step(dirn, n, steps):
        far = n >= 4
        block = (t + (2 if far else 3 if dirn == 0 else 1)) % 4
        k = c * 16 + block * 4 + CHUNKS[dirn][2 * (n - 4) if far else n]
        onward = 1 if dirn == 0 else 15
        cw_copy(dirn, n, k, sibling).wait_recv()
        if steps < 3:
            cw_copy(dirn, n, k, at_z((z + onward) % 16)).start()
        if steps == 0 and n in (0, 2):
            cw_copy(dirn, 4 + n // 2, k, at_z((z + 4 * onward) % 16)).start()
        cw_sibling(k).start()

    def tick(s):
        for chip in range(4):
            for dirn, steps in ((0, chip), (1, 3 - chip)):
                for n, start in enumerate(STARTS):
                    if start + 5 * steps == s:
                        @pl.when(l == chip)
                        def _():
                            cw_step(dirn, n, steps)

    def codes_of(h, tt):
        k = h * 16 + tt * 4
        return jnp.concatenate([cw[k], cw[k + 1]], axis=0)

    def policy_of(h, tt):
        k = h * 16 + tt * 4 + 2
        return jnp.concatenate([cw[k], cw[k + 1]], axis=0)

    def sibling_chunks(tt, first):
        for chunk in (first, first + 1):
            k = (1 - c) * 16 + tt * 4 + chunk
            cw_sibling(k).wait_recv()

    def gw_part(s):
        tt = (t + s) % 4
        gk_done(tt, s == 2)
        g = gk[tt].reshape(512, 256)
        gwx_send[tt] = jnp.dot(xt[1 - c], g, preferred_element_type=F32).astype(BF16).reshape(2, 128, 256)
        remote(gwx_send.at[tt], gwx_recv.at[tt], gwx_s, gwx_r.at[tt], sibling).start()
        gwp[tt] = jnp.dot(xt[c], g, preferred_element_type=F32).reshape(2, 128, 256)

    def gw_first(tt):
        remote(gwx_send.at[tt], gwx_recv.at[tt], gwx_s, gwx_r.at[tt], sibling).wait_recv()
        for q in range(2):
            gwp[tt, q] = gwp[tt, q] + gwx_recv[tt, q].astype(F32)
            d = tree_place(tt, q)
            down = among(d, 9, 11, 13)

            @pl.when(among(d, 2, 4, 6, 8) | down)
            def _():
                gw_send[tt, q] = gwp[tt, q].astype(BF16)
                remote(
                    gw_send.at[tt, q], gw_a.at[tt, q], gw_s.at[tt, q, 2], gwa_r.at[tt, q],
                    tree_device(jnp.where(down, 15, 1), q),
                ).start()

    def gw_add_a(tt, q):
        remote(gw_send.at[tt, q], gw_a.at[tt, q], gw_s.at[tt, q, 2], gwa_r.at[tt, q], sibling).wait_recv()
        gwp[tt, q] = gwp[tt, q] + gw_a[tt, q].astype(F32)

    def gw_second(tt):
        for q in range(2):
            d = tree_place(tt, q)

            @pl.when(among(d, 3, 7, 10, 14))
            def _():
                gw_add_a(tt, q)
                gw_send[tt, q] = gwp[tt, q].astype(BF16)
                dz = jnp.where(d == 10, 14, jnp.where(d == 14, 15, 2))
                remote(
                    gw_send.at[tt, q], gw_b.at[tt, q], gw_s.at[tt, q, 2], gwb_r.at[tt, q], tree_device(dz, q)
                ).start()

    def gw_third(tt):
        for q in range(2):
            d = tree_place(tt, q)

            @pl.when(is_final(d))
            def _():
                @pl.when(among(d, 1, 5, 12))
                def _():
                    gw_add_a(tt, q)

                @pl.when(among(d, 1, 5, 12, 15))
                def _():
                    remote(
                        gw_send.at[tt, q], gw_b.at[tt, q], gw_s.at[tt, q, 2], gwb_r.at[tt, q], sibling
                    ).wait_recv()
                    gwp[tt, q] = gwp[tt, q] + gw_b[tt, q].astype(F32)

                gw_send[tt, q] = gwp[tt, q].astype(BF16)
                slot = jnp.where(d == 1, 1, jnp.where(d == 5, 2, jnp.where(d == 12, 3, jnp.where(d == 15, 4, 0))))
                for e in range(2):
                    j = 2 * q + e

                    @pl.when(is_self(tt, j))
                    def _():
                        gw_fin[0] = gw_send[tt, q, e * 64 : (e + 1) * 64]

                    @pl.when(jnp.logical_not(is_self(tt, j)))
                    def _():
                        remote(
                            gw_send.at[tt, q, pl.ds(e * 64, 64)], gw_fin.at[slot], gw_s.at[tt, q, e],
                            fin_r.at[slot], final_device(tt, j),
                        ).start()

    def ref_part(tt):
        rows = jnp.concatenate([slab[0].reshape(512, 256), slab[1].reshape(512, 256)], axis=1)
        both = jnp.concatenate([codes_of(0, tt), codes_of(1, tt)], axis=0)
        out = jnp.dot(rows, both, preferred_element_type=F32)
        part[tt] = out.astype(BF16).reshape(16, 32, 256)
        for s in range(1, 4):
            aa = (a + s) % 4
            remote(part.at[tt, pl.ds(aa * 4, 4)], rs1.at[tt, s - 1], rs1_s, rs1_r.at[tt, s], plane(aa, b)).start()

    def ref_second(tt):
        total = part[tt, pl.ds(a * 4, 4)].astype(F32)
        for s in range(1, 4):
            remote(rs1.at[tt, s - 1], rs1.at[tt, s - 1], rs1_s, rs1_r.at[tt, s], sibling).wait_recv()
            total = total + rs1[tt, s - 1].astype(F32)
        rs1_own[tt] = total.astype(BF16)
        for s in range(1, 4):
            bb = (b + s) % 4
            remote(rs1_own.at[tt, bb], rs2.at[tt, s - 1], rs2_s, rs2_r.at[tt, s], plane(a, bb)).start()

    mine = pl.ds(pl.multiple_of(t * 32, 32), 32)

    def ref_third(s):
        tt = (t + s) % 4
        total = rs1_own[tt, b].astype(F32)
        for q in range(1, 4):
            remote(rs2.at[tt, q - 1], rs2.at[tt, q - 1], rs2_s, rs2_r.at[tt, q], sibling).wait_recv()
            total = total + rs2[tt, q - 1].astype(F32)
        keys_part[tt] = total.astype(BF16)
        if isinstance(s, int) and s == 0:
            keys_out[mine, :] = keys_part[t]
        else:
            remote(keys_part.at[tt], keys_out.at[mine], kz_s, kz_r, (o, i, tt)).start()

    def tokens_done():
        for h in range(2):
            remote(
                slab.at[h, pl.ds(0, 15)], slab.at[h, pl.ds(0, 15)], tok_s, tok_r.at[h], sibling
            ).wait_recv()
        for h in range(2):
            xt[h] = slab[h].reshape(512, 256).T

    first = jnp.where(l < 2, 3, 1)
    second = 4 - first

    def ref(s):
        tt = (t + s) % 4
        sibling_chunks(tt, 0)
        ref_part(tt)

    def gt_cols(h, q):
        return pl.ds(pl.multiple_of(slice_cols + h * 1024 + q * 128, 128), 128)

    half = jnp.where(l < 2, 0, 1)

    def grad_tokens(q):
        for tt in range(4):
            cw_sibling((1 - c) * 16 + tt * 4 + 2 + q).wait_recv()

        @pl.loop(0, 2)
        def _(j):
            acc = jnp.zeros((256, 256), F32)
            for tt in range(4):
                w = jnp.concatenate([cw[tt * 4 + 2 + q], cw[16 + tt * 4 + 2 + q]], axis=0)
                g = gk[tt, pl.ds(j * 8, 8)].reshape(256, 256)
                acc = acc + lax.dot_general(g, w, (((1,), (1,)), ((), ())), preferred_element_type=F32)
            out = acc.astype(BF16)
            for h in range(2):
                gt_send[q, h, pl.ds(j * 8, 8)] = out[:, h * 128 : (h + 1) * 128].reshape(8, 32, 128)

    def gt_own(n, q, h):
        return pltpu.make_async_copy(gt_send.at[q, h, me], gt_out.at[:, gt_cols(h, q)], load_s.at[2 * n + h])

    def gt_sends(n, q):
        @pl.loop(1, 16)
        def _(s):
            k = (me + s) % 16
            for h in range(2):
                remote(
                    gt_send.at[q, h, k], gt_out.at[:, gt_cols(h, q)], gt_s, gt_r, plane(k // 4, k % 4)
                ).start()

        for h in range(2):
            gt_own(n, q, h).start()

    gk_second(t)
    tick(0)
    heard_near()
    gk_exchanged(1)
    gk_exchanged(3)
    gk_passed_on()
    tick(2)
    tick(4)
    tick(5)
    gk_second((t + 3) % 4)
    gk_second((t + 1) % 4)
    tick(7)
    tokens_done()
    gk_exchanged(2)
    tick(8)
    tick(9)
    gw_part(0)
    tick(10)
    ref(0)
    tick(12)
    tick(13)
    gw_part(3)
    gw_first(t)
    tick(14)
    gw_part(1)
    tick(15)
    gw_part(2)
    gw_first((t + 3) % 4)
    tick(17)
    gw_first((t + 1) % 4)
    ref(first)
    tick(18)
    gw_first((t + 2) % 4)
    tick(19)
    ref_second(t)
    ref(second)
    tick(22)
    tick(23)
    ref(2)
    ref_second((t + first) % 4)
    gw_second(t)
    gw_second((t + 3) % 4)
    gw_second((t + 1) % 4)
    gw_second((t + 2) % 4)
    grad_tokens(half)
    gt_sends(0, half)
    ref_second((t + second) % 4)
    ref_third(0)
    ref_third(first)
    heard_far()
    tick(28)
    grad_tokens(1 - half)
    ref_second((t + 2) % 4)
    gt_sends(1, 1 - half)
    gw_third(t)
    gw_third((t + 3) % 4)
    gw_third((t + 1) % 4)
    gw_third((t + 2) % 4)
    ref_third(second)
    ref_third(2)

    src_self = (2 * (l % 2) + x // 2 == y) & (y * 2 + l // 2 == i)
    total = jnp.zeros((64, 256), F32)
    for slot in range(5):
        def arrived():
            remote(gw_fin.at[slot], gw_fin.at[slot], gw_s.at[0, 0, 0], fin_r.at[slot], sibling).wait_recv()

        if slot == 0:
            pl.when(jnp.logical_not(src_self))(arrived)
        else:
            arrived()
        total = total + gw_fin[slot].astype(F32)
    gw_out[...] = total * lax.rsqrt(jnp.full((1, 1), 16384.0, F32))

    for n, q in ((0, half), (1, 1 - half)):
        for h in range(2):
            gt_own(n, q, h).wait()
    gt_all = gt_out.at[:, pl.ds(0, 30 * 256)]
    remote(gt_all, gt_all, gt_s, gt_r, sibling).wait_recv()
    remote(keys_out.at[pl.ds(0, 96)], keys_out.at[pl.ds(0, 96)], kz_s, kz_r, sibling).wait()
    remote(gk_relay, gk_relay, relay_s, relay_r.at[0], sibling).wait_send()
    remote(gkeys_v.at[pl.ds(0, 96)], gkeys_v.at[pl.ds(0, 96)], gkz_s, gkz_r.at[0], sibling).wait_send()
    remote(gt_all, gt_all, tok_s, tok_r.at[0], sibling).wait_send()
    remote(gt_all, gt_all, gt_s, gt_r, sibling).wait_send()
    remote(gk.at[0, pl.ds(0, 9)], gk.at[0, pl.ds(0, 9)], gk1_s, gk1_r.at[0, 0], sibling).wait_send()
    remote(gk.at[0, pl.ds(0, 15)], gk.at[0, pl.ds(0, 15)], gkd_s, gkd_r, sibling).wait_send()
    remote(rs1.at[pl.ds(0, 3)], rs1.at[pl.ds(0, 3)], gk2_s, gk2_r.at[0, 0], sibling).wait_send()
    remote(part.at[pl.ds(0, 3)], part.at[pl.ds(0, 3)], rs1_s, rs1_r.at[0, 0], sibling).wait_send()
    remote(rs2, rs2, rs2_s, rs2_r.at[0, 0], sibling).wait_send()
    for dirn, steps in ((0, l), (1, 3 - l)):
        for sent, here in ((4, steps == 3), (8, steps == 0), (6, among(steps, 1, 2))):
            @pl.when(here)
            def _():
                rows = cw.at[pl.ds(0, sent)]
                remote(rows, rows, cw_s.at[dirn], cw_r.at[dirn, 0], sibling).wait_send()
    remote(cw.at[pl.ds(0, 16)], cw.at[pl.ds(0, 16)], cws_s, cws_r.at[0], sibling).wait_send()
    remote(gwx_send, gwx_send, gwx_s, gwx_r.at[0], sibling).wait_send()
    for tt in range(4):
        for q in range(2):
            final = is_final(tree_place(tt, q))

            @pl.when(jnp.logical_not(final))
            def _():
                remote(gw_send.at[tt, q], gw_send.at[tt, q], gw_s.at[tt, q, 2], gwa_r.at[tt, q], sibling).wait_send()

            for e in range(2):
                rows = gw_send.at[tt, q, pl.ds(e * 64, 64)]

                @pl.when(final & jnp.logical_not(is_self(tt, 2 * q + e)))
                def _():
                    remote(rows, rows, gw_s.at[tt, q, e], gwa_r.at[tt, q], sibling).wait_send()


def copy_kernel(keys, gw, gt, keys_out, gw_out, gt_out, keys_v, gw_v, gt_v, in_s, out_s):
    rows = ((gt, gt_v, gt_out), (keys, keys_v, keys_out), (gw, gw_v, gw_out))
    loads = [pltpu.make_async_copy(src, mid, in_s.at[n]) for n, (src, mid, _) in enumerate(rows)]
    stores = [pltpu.make_async_copy(mid, dst, out_s.at[n]) for n, (_, mid, dst) in enumerate(rows)]
    for load in loads:
        load.start()
    for load, store in zip(loads, stores):
        load.wait()
        store.start()
    for store in stores:
        store.wait()


def body(tokens, ref_codes, ref_scales, policy_weight, grad_keys):
    vmem = pl.BlockSpec(memory_space=pltpu.VMEM)
    hbm = pl.BlockSpec(memory_space=pltpu.HBM)
    dma = pltpu.SemaphoreType.DMA
    outs = pl.pallas_call(
        kernel,
        out_shape=(
            jax.ShapeDtypeStruct((128, 256), BF16),
            jax.ShapeDtypeStruct((64, 256), F32),
            jax.ShapeDtypeStruct((32, 8192), BF16),
        ),
        in_specs=[hbm] * 5,
        out_specs=[vmem, vmem, hbm],
        scratch_shapes=[
            pltpu.VMEM((2, 128, 256), BF16),
            pltpu.VMEM((8, 256), F32),
            pltpu.VMEM((128, 256), BF16),
            pltpu.VMEM((2, 16, 32, 256), BF16),
            pltpu.VMEM((4, 16, 32, 256), BF16),
            pltpu.VMEM((32, 128, 256), BF16),
            pltpu.VMEM((2, 256, 512), BF16),
            pltpu.VMEM((4, 16, 32, 256), BF16),
            pltpu.VMEM((4, 3, 4, 32, 256), BF16),
            pltpu.VMEM((4, 4, 32, 256), BF16),
            pltpu.VMEM((4, 3, 32, 256), BF16),
            pltpu.VMEM((4, 32, 256), BF16),
            pltpu.VMEM((4, 2, 128, 256), BF16),
            pltpu.VMEM((4, 2, 128, 256), BF16),
            pltpu.VMEM((4, 2, 128, 256), F32),
            pltpu.VMEM((4, 2, 128, 256), BF16),
            pltpu.VMEM((4, 2, 128, 256), BF16),
            pltpu.VMEM((4, 2, 128, 256), BF16),
            pltpu.VMEM((5, 64, 256), BF16),
            pltpu.VMEM((2, 2, 16, 32, 128), BF16),
            dma((7,)),
            dma, dma((2,)),
            dma, dma((4,)),
            dma, dma((4, 4)), dma, dma((4, 4)), dma, dma,
            dma((2,)), dma((2, 6)), dma, dma((16,)),
            dma, dma((4, 4)), dma, dma((4, 4)),
            dma, dma,
            dma, dma((4,)),
            dma((4, 2, 3)), dma((4, 2)), dma((4, 2)), dma((5,)),
            dma, dma,
            pltpu.SemaphoreType.REGULAR, pltpu.SemaphoreType.REGULAR,
            pltpu.VMEM((2, 16, 256), BF16),
            dma, dma((2,)), dma((2,)),
        ],
        compiler_params=pltpu.CompilerParams(
            collective_id=0, has_side_effects=True, vmem_limit_bytes=64 * 1024 * 1024 - 256 * 1024
        ),
        cost_estimate=pl.CostEstimate(flops=1_700_000_000, bytes_accessed=4_000_000, transcendentals=0),
    )(tokens, ref_codes, ref_scales, policy_weight, grad_keys)
    return pl.pallas_call(
        copy_kernel,
        out_shape=tuple(jax.ShapeDtypeStruct(out.shape, out.dtype) for out in outs),
        in_specs=[hbm] * 3,
        out_specs=[hbm] * 3,
        scratch_shapes=[pltpu.VMEM(out.shape, out.dtype) for out in outs] + [dma((3,)), dma((3,))],
        compiler_params=pltpu.CompilerParams(vmem_limit_bytes=62 * 1024 * 1024),
    )(*outs)


def solution(mesh):
    return jax.shard_map(
        body,
        mesh=mesh,
        in_specs=(
            P(("outer", "inner", "tensor"), None),
            P("inner", None, "tensor"),
            P("inner", "tensor"),
            P("inner", "tensor"),
            P(("outer", "inner"), "tensor"),
        ),
        out_specs=(
            P(("outer", "inner"), "tensor"),
            P(("outer", "inner"), "tensor"),
            P(("outer", "inner", "tensor"), None),
        ),
        check_vma=False,
    )
```

```python
import jax
import jax.numpy as jnp
from jax import lax
from jax.experimental import pallas as pl
from jax.experimental.pallas import tpu as pltpu
from jax.sharding import PartitionSpec as P

MESH = pl.DeviceIdType.MESH
F32 = jnp.float32
BF16 = jnp.bfloat16


CHUNKS = ((0, 1, 2, 3), (1, 0, 3, 2))
STARTS = (0, 2, 4, 7, 8, 13)


def remote(src, dst, send_sem, recv_sem, device):
    return pltpu.make_async_remote_copy(
        src_ref=src,
        dst_ref=dst,
        send_sem=send_sem,
        recv_sem=recv_sem,
        device_id=device,
        device_id_type=MESH,
    )


def among(value, *choices):
    found = value == choices[0]
    for choice in choices[1:]:
        found = found | (value == choice)
    return found


def kernel(
    tok, codes, scales, policy, gkeys,
    keys_out, gw_out, gt_out,
    codes_v, scales_v, gkeys_v, slab, gk, cw, xt, part, rs1, rs1_own, rs2, keys_part,
    gwx_send, gwx_recv, gwp, gw_send, gw_a, gw_b, gw_fin, gt_send,
    load_s, tok_s, tok_r, gkz_s, gkz_r, gk1_s, gk1_r, gk2_s, gk2_r, gkd_s, gkd_r, cw_s, cw_r, cws_s, cws_r,
    rs1_s, rs1_r, rs2_s, rs2_r, kz_s, kz_r, gwx_s, gwx_r, gw_s, gwa_r, gwb_r, fin_r, gt_s, gt_r,
    near_in, far_in, gk_relay, relay_s, relay_r, passed_r,
):
    o = lax.axis_index("outer")
    i = lax.axis_index("inner")
    t = lax.axis_index("tensor")
    y, l = o // 4, o % 4
    x, c = i // 2, i % 2
    z = t * 4 + l
    a = jnp.where(c == 0, x, y)
    b = jnp.where(c == 0, y, x)
    me = a * 4 + b

    def place(aa, bb):
        yy = jnp.where(c == 0, bb, aa)
        xx = jnp.where(c == 0, aa, bb)
        return yy, xx

    def plane(aa, bb):
        yy, xx = place(aa, bb)
        return (yy * 4 + l, xx * 2 + c, t)

    def at_z(zz):
        return (y * 4 + zz % 4, i, zz // 4)

    sibling = (o, x * 2 + (1 - c), t)

    own_l = 2 * c + y // 2

    def final_device(tt, j):
        return (x * 4 + own_l, (2 * (y % 2) + j // 2) * 2 + j % 2, tt)

    def tree_place(tt, q):
        d = (tt * 4 + own_l + 16 - z) % 16
        return d if q == 0 else (16 - d) % 16

    def tree_device(dz, q):
        return at_z((z + (dz if q == 0 else 16 - dz)) % 16)

    def is_final(d):
        return among(d, 0, 1, 5, 12, 15)

    def is_self(tt, j):
        fo, fi, ft = final_device(tt, j)
        return (fo == o) & (fi == i) & (ft == t)

    barrier = pltpu.get_barrier_semaphore()

    def greet(device):
        pl.semaphore_signal(barrier, inc=1, device_id=device, device_id_type=MESH)

    @pl.loop(1, 16)
    def _(s):
        k = (me + s) % 16
        greet(plane(k // 4, k % 4))

    greet(sibling)
    for dz in (1, 15, 4, 12):
        greet(at_z((z + dz) % 16))

    slice_cols = x * 2048 + y * 256
    loads = [
        pltpu.make_async_copy(gkeys, gkeys_v, load_s.at[0]),
        pltpu.make_async_copy(codes.at[pl.ds(2 * y, 2)], codes_v, load_s.at[1]),
        pltpu.make_async_copy(scales, scales_v, load_s.at[2]),
    ]
    for h in range(2):
        loads.append(
            pltpu.make_async_copy(
                policy.at[pl.ds(pl.multiple_of(y * 256 + h * 128, 128), 128)],
                cw.at[c * 16 + t * 4 + 2 + h],
                load_s.at[3 + h],
            )
        )
        loads.append(
            pltpu.make_async_copy(
                tok.at[:, pl.ds(pl.multiple_of(slice_cols + h * 1024, 256), 256)],
                slab.at[h, me],
                load_s.at[5 + h],
            )
        )
    for load in loads:
        load.start()
    for load in loads:
        load.wait()
    for h in range(2):
        cw[c * 16 + t * 4 + h] = (codes_v[h].astype(F32) * scales_v[pl.ds(2 * y + h, 1), :]).astype(BF16)
    gk[t, me] = gkeys_v[pl.ds(pl.multiple_of(t * 32, 32), 32), :]

    pl.semaphore_wait(barrier, 20)

    def tell(sem, device):
        pl.semaphore_signal(sem, inc=1, device_id=device, device_id_type=MESH)

    tell(near_in, sibling)
    for dz in (1, 15, 4, 12):
        tell(near_in, at_z((z + dz) % 16))

    def heard_near():
        pl.semaphore_wait(near_in, 5)
        for dz in (1, 15, 4, 12, 5, 11):
            tell(far_in, at_z((z + dz) % 16))

    def heard_far():
        pl.semaphore_wait(far_in, 6)

    def cw_copy(dirn, n, k, device):
        return remote(cw.at[k], cw.at[k], cw_s.at[dirn], cw_r.at[dirn, n], device)

    def cw_sibling(k):
        return remote(cw.at[k], cw.at[k], cws_s, cws_r.at[k % 16], sibling)

    def gk_send(s):
        tt = (t + s) % 4
        remote(
            gkeys_v.at[pl.ds(pl.multiple_of(tt * 32, 32), 32)], gk.at[t, me], gkz_s, gkz_r.at[s], (o, i, tt)
        ).start()

    gk_send(1)
    gk_send(3)

    def relay_rows(n):
        return pl.ds(pl.multiple_of((t + 2) % 4 * 32 + n * 16, 16), 16)

    for n, s in ((0, 1), (1, 3)):
        remote(gkeys_v.at[relay_rows(n)], gk_relay.at[n], gkz_s, relay_r.at[n], (o, i, (t + s) % 4)).start()

    def gk_landing(tt, n):
        return gk.at[tt, me, pl.ds(n * 16, 16)]

    def gk_passed_on():
        for n, s in ((0, 1), (1, 3)):
            remote(gk_relay.at[n], gk_relay.at[n], gkz_s, relay_r.at[n], sibling).wait_recv()
            remote(
                gk_relay.at[n], gk_landing((t + 4 - s) % 4, n), relay_s, passed_r.at[n], (o, i, (t + s) % 4)
            ).start()

    def gk_first(tt):
        for s in range(1, 4):
            remote(gk.at[tt, me], gk.at[tt, me], gk1_s, gk1_r.at[tt, s], plane(a, (b + s) % 4)).start()

    def gk_second(tt):
        for s in range(1, 4):
            k = a * 4 + (b + 4 - s) % 4
            remote(gk.at[tt, k], gk.at[tt, k], gk1_s, gk1_r.at[tt, s], sibling).wait_recv()
        rows = gk.at[tt, pl.ds(a * 4, 4)]
        for s in range(1, 4):
            remote(rows, rows, gk2_s, gk2_r.at[tt, s], plane((a + s) % 4, b)).start()

    def gk_done(tt, direct=False):
        if direct:
            rows = gk.at[tt, pl.ds(0, 15)]
            remote(rows, rows, gkd_s, gkd_r, sibling).wait_recv()
            return
        for s in range(1, 4):
            rows = gk.at[tt, pl.ds((a + 4 - s) % 4 * 4, 4)]
            remote(rows, rows, gk2_s, gk2_r.at[tt, s], sibling).wait_recv()

    def gk_direct(tt):
        @pl.loop(1, 16)
        def _(s):
            k = (me + s) % 16
            remote(gk.at[tt, me], gk.at[tt, me], gkd_s, gkd_r, plane(k // 4, k % 4)).start()

    def gk_exchanged(s):
        tt = (t + 4 - s) % 4
        if s == 2:
            for n in range(2):
                remote(gk_landing(tt, n), gk_landing(tt, n), gkz_s, passed_r.at[n], sibling).wait_recv()
            gk_direct(tt)
        else:
            remote(gk.at[tt, me], gk.at[tt, me], gkz_s, gkz_r.at[s], sibling).wait_recv()
            gk_first(tt)

    gk_first(t)

    own = c * 16 + t * 4
    for n in range(4):
        @pl.when(l == 3)
        def _():
            cw_copy(0, n, own + CHUNKS[0][n], at_z((z + 1) % 16)).start()

        @pl.when(l == 0)
        def _():
            cw_copy(1, n, own + CHUNKS[1][n], at_z((z + 15) % 16)).start()

    @pl.loop(1, 16)
    def _(s):
        k = (me + s) % 16
        yy, xx = place(k // 4, k % 4)
        for h in range(2):
            cols = pl.ds(pl.multiple_of(xx * 2048 + yy * 256 + h * 1024, 256), 256)
            remote(tok.at[:, cols], slab.at[h, me], tok_s, tok_r.at[h], plane(k // 4, k % 4)).start()

    for chunk in range(4):
        cw_sibling(own + chunk).start()

    def cw_step(dirn, n, steps):
        far = n >= 4
        block = (t + (2 if far else 3 if dirn == 0 else 1)) % 4
        k = c * 16 + block * 4 + CHUNKS[dirn][2 * (n - 4) if far else n]
        onward = 1 if dirn == 0 else 15
        cw_copy(dirn, n, k, sibling).wait_recv()
        if steps < 3:
            cw_copy(dirn, n, k, at_z((z + onward) % 16)).start()
        if steps == 0 and n in (0, 2):
            cw_copy(dirn, 4 + n // 2, k, at_z((z + 4 * onward) % 16)).start()
        cw_sibling(k).start()

    def tick(s):
        for chip in range(4):
            for dirn, steps in ((0, chip), (1, 3 - chip)):
                for n, start in enumerate(STARTS):
                    if start + 5 * steps == s:
                        @pl.when(l == chip)
                        def _():
                            cw_step(dirn, n, steps)

    def codes_of(h, tt):
        k = h * 16 + tt * 4
        return jnp.concatenate([cw[k], cw[k + 1]], axis=0)

    def policy_of(h, tt):
        k = h * 16 + tt * 4 + 2
        return jnp.concatenate([cw[k], cw[k + 1]], axis=0)

    def sibling_chunks(tt, first):
        for chunk in (first, first + 1):
            k = (1 - c) * 16 + tt * 4 + chunk
            cw_sibling(k).wait_recv()

    def gw_part(s):
        tt = (t + s) % 4
        gk_done(tt, s == 2)
        g = gk[tt].reshape(512, 256)
        gwx_send[tt] = jnp.dot(xt[1 - c], g, preferred_element_type=F32).astype(BF16).reshape(2, 128, 256)
        remote(gwx_send.at[tt], gwx_recv.at[tt], gwx_s, gwx_r.at[tt], sibling).start()
        gwp[tt] = jnp.dot(xt[c], g, preferred_element_type=F32).reshape(2, 128, 256)

    def gw_first(tt):
        remote(gwx_send.at[tt], gwx_recv.at[tt], gwx_s, gwx_r.at[tt], sibling).wait_recv()
        for q in range(2):
            gwp[tt, q] = gwp[tt, q] + gwx_recv[tt, q].astype(F32)
            d = tree_place(tt, q)
            down = among(d, 9, 11, 13)

            @pl.when(among(d, 2, 4, 6, 8) | down)
            def _():
                gw_send[tt, q] = gwp[tt, q].astype(BF16)
                remote(
                    gw_send.at[tt, q], gw_a.at[tt, q], gw_s.at[tt, q, 2], gwa_r.at[tt, q],
                    tree_device(jnp.where(down, 15, 1), q),
                ).start()

    def gw_add_a(tt, q):
        remote(gw_send.at[tt, q], gw_a.at[tt, q], gw_s.at[tt, q, 2], gwa_r.at[tt, q], sibling).wait_recv()
        gwp[tt, q] = gwp[tt, q] + gw_a[tt, q].astype(F32)

    def gw_second(tt):
        for q in range(2):
            d = tree_place(tt, q)

            @pl.when(among(d, 3, 7, 10, 14))
            def _():
                gw_add_a(tt, q)
                gw_send[tt, q] = gwp[tt, q].astype(BF16)
                dz = jnp.where(d == 10, 14, jnp.where(d == 14, 15, 2))
                remote(
                    gw_send.at[tt, q], gw_b.at[tt, q], gw_s.at[tt, q, 2], gwb_r.at[tt, q], tree_device(dz, q)
                ).start()

    def gw_third(tt):
        for q in range(2):
            d = tree_place(tt, q)

            @pl.when(is_final(d))
            def _():
                @pl.when(among(d, 1, 5, 12))
                def _():
                    gw_add_a(tt, q)

                @pl.when(among(d, 1, 5, 12, 15))
                def _():
                    remote(
                        gw_send.at[tt, q], gw_b.at[tt, q], gw_s.at[tt, q, 2], gwb_r.at[tt, q], sibling
                    ).wait_recv()
                    gwp[tt, q] = gwp[tt, q] + gw_b[tt, q].astype(F32)

                gw_send[tt, q] = gwp[tt, q].astype(BF16)
                slot = jnp.where(d == 1, 1, jnp.where(d == 5, 2, jnp.where(d == 12, 3, jnp.where(d == 15, 4, 0))))
                for e in range(2):
                    j = 2 * q + e

                    @pl.when(is_self(tt, j))
                    def _():
                        gw_fin[0] = gw_send[tt, q, e * 64 : (e + 1) * 64]

                    @pl.when(jnp.logical_not(is_self(tt, j)))
                    def _():
                        remote(
                            gw_send.at[tt, q, pl.ds(e * 64, 64)], gw_fin.at[slot], gw_s.at[tt, q, e],
                            fin_r.at[slot], final_device(tt, j),
                        ).start()

    def ref_part(tt):
        rows = jnp.concatenate([slab[0].reshape(512, 256), slab[1].reshape(512, 256)], axis=1)
        both = jnp.concatenate([codes_of(0, tt), codes_of(1, tt)], axis=0)
        out = jnp.dot(rows, both, preferred_element_type=F32)
        part[tt] = out.astype(BF16).reshape(16, 32, 256)
        for s in range(1, 4):
            aa = (a + s) % 4
            remote(part.at[tt, pl.ds(aa * 4, 4)], rs1.at[tt, s - 1], rs1_s, rs1_r.at[tt, s], plane(aa, b)).start()

    def ref_second(tt):
        total = part[tt, pl.ds(a * 4, 4)].astype(F32)
        for s in range(1, 4):
            remote(rs1.at[tt, s - 1], rs1.at[tt, s - 1], rs1_s, rs1_r.at[tt, s], sibling).wait_recv()
            total = total + rs1[tt, s - 1].astype(F32)
        rs1_own[tt] = total.astype(BF16)
        for s in range(1, 4):
            bb = (b + s) % 4
            remote(rs1_own.at[tt, bb], rs2.at[tt, s - 1], rs2_s, rs2_r.at[tt, s], plane(a, bb)).start()

    mine = pl.ds(pl.multiple_of(t * 32, 32), 32)

    def ref_third(s):
        tt = (t + s) % 4
        total = rs1_own[tt, b].astype(F32)
        for q in range(1, 4):
            remote(rs2.at[tt, q - 1], rs2.at[tt, q - 1], rs2_s, rs2_r.at[tt, q], sibling).wait_recv()
            total = total + rs2[tt, q - 1].astype(F32)
        keys_part[tt] = total.astype(BF16)
        if isinstance(s, int) and s == 0:
            keys_out[mine, :] = keys_part[t]
        else:
            remote(keys_part.at[tt], keys_out.at[mine], kz_s, kz_r, (o, i, tt)).start()

    def tokens_done():
        for h in range(2):
            remote(
                slab.at[h, pl.ds(0, 15)], slab.at[h, pl.ds(0, 15)], tok_s, tok_r.at[h], sibling
            ).wait_recv()
        for h in range(2):
            xt[h] = slab[h].reshape(512, 256).T

    first = jnp.where(l < 2, 3, 1)
    second = 4 - first

    def ref(s):
        tt = (t + s) % 4
        sibling_chunks(tt, 0)
        ref_part(tt)

    def gt_cols(h, q):
        return pl.ds(pl.multiple_of(slice_cols + h * 1024 + q * 128, 128), 128)

    half = jnp.where(l < 2, 0, 1)

    def grad_tokens(q):
        for tt in range(4):
            cw_sibling((1 - c) * 16 + tt * 4 + 2 + q).wait_recv()

        @pl.loop(0, 2)
        def _(j):
            acc = jnp.zeros((256, 256), F32)
            for tt in range(4):
                w = jnp.concatenate([cw[tt * 4 + 2 + q], cw[16 + tt * 4 + 2 + q]], axis=0)
                g = gk[tt, pl.ds(j * 8, 8)].reshape(256, 256)
                acc = acc + lax.dot_general(g, w, (((1,), (1,)), ((), ())), preferred_element_type=F32)
            out = acc.astype(BF16)
            for h in range(2):
                gt_send[q, h, pl.ds(j * 8, 8)] = out[:, h * 128 : (h + 1) * 128].reshape(8, 32, 128)

    def gt_own(n, q, h):
        return pltpu.make_async_copy(gt_send.at[q, h, me], gt_out.at[:, gt_cols(h, q)], load_s.at[2 * n + h])

    def gt_sends(n, q):
        @pl.loop(1, 16)
        def _(s):
            k = (me + s) % 16
            for h in range(2):
                remote(
                    gt_send.at[q, h, k], gt_out.at[:, gt_cols(h, q)], gt_s, gt_r, plane(k // 4, k % 4)
                ).start()

        for h in range(2):
            gt_own(n, q, h).start()

    gk_second(t)
    tick(0)
    heard_near()
    gk_exchanged(1)
    gk_exchanged(3)
    gk_passed_on()
    tick(2)
    tick(4)
    tick(5)
    gk_second((t + 3) % 4)
    gk_second((t + 1) % 4)
    tick(7)
    tokens_done()
    gk_exchanged(2)
    tick(8)
    tick(9)
    gw_part(0)
    tick(10)
    ref(0)
    tick(12)
    tick(13)
    gw_part(3)
    gw_first(t)
    tick(14)
    gw_part(1)
    tick(15)
    gw_part(2)
    gw_first((t + 3) % 4)
    tick(17)
    gw_first((t + 1) % 4)
    ref(first)
    tick(18)
    gw_first((t + 2) % 4)
    tick(19)
    ref_second(t)
    ref(second)
    tick(22)
    tick(23)
    ref(2)
    ref_second((t + first) % 4)
    gw_second(t)
    gw_second((t + 3) % 4)
    gw_second((t + 1) % 4)
    gw_second((t + 2) % 4)
    grad_tokens(half)
    gt_sends(0, half)
    ref_second((t + second) % 4)
    ref_third(0)
    ref_third(first)
    heard_far()
    tick(28)
    grad_tokens(1 - half)
    gt_sends(1, 1 - half)
    ref_second((t + 2) % 4)
    gw_third(t)
    gw_third((t + 3) % 4)
    gw_third((t + 1) % 4)
    gw_third((t + 2) % 4)
    ref_third(second)
    ref_third(2)

    src_self = (2 * (l % 2) + x // 2 == y) & (y * 2 + l // 2 == i)
    total = jnp.zeros((64, 256), F32)
    for slot in range(5):
        def arrived():
            remote(gw_fin.at[slot], gw_fin.at[slot], gw_s.at[0, 0, 0], fin_r.at[slot], sibling).wait_recv()

        if slot == 0:
            pl.when(jnp.logical_not(src_self))(arrived)
        else:
            arrived()
        total = total + gw_fin[slot].astype(F32)
    gw_out[...] = total * lax.rsqrt(jnp.full((1, 1), 16384.0, F32))

    for n, q in ((0, half), (1, 1 - half)):
        for h in range(2):
            gt_own(n, q, h).wait()
    gt_all = gt_out.at[:, pl.ds(0, 30 * 256)]
    remote(gt_all, gt_all, gt_s, gt_r, sibling).wait_recv()
    remote(keys_out.at[pl.ds(0, 96)], keys_out.at[pl.ds(0, 96)], kz_s, kz_r, sibling).wait()
    remote(gk_relay, gk_relay, relay_s, relay_r.at[0], sibling).wait_send()
    remote(gkeys_v.at[pl.ds(0, 96)], gkeys_v.at[pl.ds(0, 96)], gkz_s, gkz_r.at[0], sibling).wait_send()
    remote(gt_all, gt_all, tok_s, tok_r.at[0], sibling).wait_send()
    remote(gt_all, gt_all, gt_s, gt_r, sibling).wait_send()
    remote(gk.at[0, pl.ds(0, 9)], gk.at[0, pl.ds(0, 9)], gk1_s, gk1_r.at[0, 0], sibling).wait_send()
    remote(gk.at[0, pl.ds(0, 15)], gk.at[0, pl.ds(0, 15)], gkd_s, gkd_r, sibling).wait_send()
    remote(rs1.at[pl.ds(0, 3)], rs1.at[pl.ds(0, 3)], gk2_s, gk2_r.at[0, 0], sibling).wait_send()
    remote(part.at[pl.ds(0, 3)], part.at[pl.ds(0, 3)], rs1_s, rs1_r.at[0, 0], sibling).wait_send()
    remote(rs2, rs2, rs2_s, rs2_r.at[0, 0], sibling).wait_send()
    for dirn, steps in ((0, l), (1, 3 - l)):
        for sent, here in ((4, steps == 3), (8, steps == 0), (6, among(steps, 1, 2))):
            @pl.when(here)
            def _():
                rows = cw.at[pl.ds(0, sent)]
                remote(rows, rows, cw_s.at[dirn], cw_r.at[dirn, 0], sibling).wait_send()
    remote(cw.at[pl.ds(0, 16)], cw.at[pl.ds(0, 16)], cws_s, cws_r.at[0], sibling).wait_send()
    remote(gwx_send, gwx_send, gwx_s, gwx_r.at[0], sibling).wait_send()
    for tt in range(4):
        for q in range(2):
            final = is_final(tree_place(tt, q))

            @pl.when(jnp.logical_not(final))
            def _():
                remote(gw_send.at[tt, q], gw_send.at[tt, q], gw_s.at[tt, q, 2], gwa_r.at[tt, q], sibling).wait_send()

            for e in range(2):
                rows = gw_send.at[tt, q, pl.ds(e * 64, 64)]

                @pl.when(final & jnp.logical_not(is_self(tt, 2 * q + e)))
                def _():
                    remote(rows, rows, gw_s.at[tt, q, e], gwa_r.at[tt, q], sibling).wait_send()


def copy_kernel(keys, gw, gt, keys_out, gw_out, gt_out, keys_v, gw_v, gt_v, in_s, out_s):
    rows = ((gt, gt_v, gt_out), (keys, keys_v, keys_out), (gw, gw_v, gw_out))
    loads = [pltpu.make_async_copy(src, mid, in_s.at[n]) for n, (src, mid, _) in enumerate(rows)]
    stores = [pltpu.make_async_copy(mid, dst, out_s.at[n]) for n, (_, mid, dst) in enumerate(rows)]
    for load in loads:
        load.start()
    for load, store in zip(loads, stores):
        load.wait()
        store.start()
    for store in stores:
        store.wait()


def body(tokens, ref_codes, ref_scales, policy_weight, grad_keys):
    vmem = pl.BlockSpec(memory_space=pltpu.VMEM)
    hbm = pl.BlockSpec(memory_space=pltpu.HBM)
    dma = pltpu.SemaphoreType.DMA
    outs = pl.pallas_call(
        kernel,
        out_shape=(
            jax.ShapeDtypeStruct((128, 256), BF16),
            jax.ShapeDtypeStruct((64, 256), F32),
            jax.ShapeDtypeStruct((32, 8192), BF16),
        ),
        in_specs=[hbm] * 5,
        out_specs=[vmem, vmem, hbm],
        scratch_shapes=[
            pltpu.VMEM((2, 128, 256), BF16),
            pltpu.VMEM((8, 256), F32),
            pltpu.VMEM((128, 256), BF16),
            pltpu.VMEM((2, 16, 32, 256), BF16),
            pltpu.VMEM((4, 16, 32, 256), BF16),
            pltpu.VMEM((32, 128, 256), BF16),
            pltpu.VMEM((2, 256, 512), BF16),
            pltpu.VMEM((4, 16, 32, 256), BF16),
            pltpu.VMEM((4, 3, 4, 32, 256), BF16),
            pltpu.VMEM((4, 4, 32, 256), BF16),
            pltpu.VMEM((4, 3, 32, 256), BF16),
            pltpu.VMEM((4, 32, 256), BF16),
            pltpu.VMEM((4, 2, 128, 256), BF16),
            pltpu.VMEM((4, 2, 128, 256), BF16),
            pltpu.VMEM((4, 2, 128, 256), F32),
            pltpu.VMEM((4, 2, 128, 256), BF16),
            pltpu.VMEM((4, 2, 128, 256), BF16),
            pltpu.VMEM((4, 2, 128, 256), BF16),
            pltpu.VMEM((5, 64, 256), BF16),
            pltpu.VMEM((2, 2, 16, 32, 128), BF16),
            dma((7,)),
            dma, dma((2,)),
            dma, dma((4,)),
            dma, dma((4, 4)), dma, dma((4, 4)), dma, dma,
            dma((2,)), dma((2, 6)), dma, dma((16,)),
            dma, dma((4, 4)), dma, dma((4, 4)),
            dma, dma,
            dma, dma((4,)),
            dma((4, 2, 3)), dma((4, 2)), dma((4, 2)), dma((5,)),
            dma, dma,
            pltpu.SemaphoreType.REGULAR, pltpu.SemaphoreType.REGULAR,
            pltpu.VMEM((2, 16, 256), BF16),
            dma, dma((2,)), dma((2,)),
        ],
        compiler_params=pltpu.CompilerParams(
            collective_id=0, has_side_effects=True, vmem_limit_bytes=64 * 1024 * 1024 - 256 * 1024
        ),
        cost_estimate=pl.CostEstimate(flops=1_700_000_000, bytes_accessed=4_000_000, transcendentals=0),
    )(tokens, ref_codes, ref_scales, policy_weight, grad_keys)
    return pl.pallas_call(
        copy_kernel,
        out_shape=tuple(jax.ShapeDtypeStruct(out.shape, out.dtype) for out in outs),
        in_specs=[hbm] * 3,
        out_specs=[hbm] * 3,
        scratch_shapes=[pltpu.VMEM(out.shape, out.dtype) for out in outs] + [dma((3,)), dma((3,))],
        compiler_params=pltpu.CompilerParams(vmem_limit_bytes=62 * 1024 * 1024),
    )(*outs)


def solution(mesh):
    return jax.shard_map(
        body,
        mesh=mesh,
        in_specs=(
            P(("outer", "inner", "tensor"), None),
            P("inner", None, "tensor"),
            P("inner", "tensor"),
            P("inner", "tensor"),
            P(("outer", "inner"), "tensor"),
        ),
        out_specs=(
            P(("outer", "inner"), "tensor"),
            P(("outer", "inner"), "tensor"),
            P(("outer", "inner", "tensor"), None),
        ),
        check_vma=False,
    )
```
